32 devices in a mesh: expert: 4 (over y, x), cuts: 8 (over z, core).
Axes of the slice: x: 2, y: 2, z: 4, core: 2. Of those that a mesh axis runs over, the one named last changes fastest.
Arguments:
- out_grad: bfloat16 [512, 6144], P('expert', 'cuts'), may hold values from -6 to 6
- gate_probs: float32 [512, 2], P('expert'), may hold values from 0.2 to 1
- expert_ids: int32 [512, 2], P('expert'), may hold values from 0 to 3, all different within a row; in each aligned block of 128 rows (0 to 127, 128 to 255, ...) at most 64 rows name the same one
- gate_pre: bfloat16 [4, 4, 64, 8192], P('expert', None, None, 'cuts'), may hold values from -6 to 6
- up_pre: bfloat16 [4, 4, 64, 8192], P('expert', None, None, 'cuts'), may hold values from -6 to 6
- w_gate: bfloat16 [4, 6144, 8192], P('expert', None, 'cuts'), may hold values from -0.109375 to 0.109375
- w_up: bfloat16 [4, 6144, 8192], P('expert', None, 'cuts'), may hold values from -0.109375 to 0.109375
- w_down: bfloat16 [4, 8192, 6144], P('expert', 'cuts'), may hold values from -0.0625 to 0.0625
Outputs:
- input_grad: bfloat16 [512, 6144], P('expert', 'cuts')
- w_down_grad: bfloat16 [4, 8192, 6144], P('expert', 'cuts')
The draws below stay inside these ranges and needn't reach their ends.
Inputs may be any that keep to these rules, and one draw needn't show every extreme that they name: `expert_ids`: each row names 2 different experts. Among the 128 tokens of one index of the expert axis no expert is named more than 64 times.
All inputs are finite; a program needn't handle non-finite values.
Results may differ from the reference program's by a relative error of at most 0.034.
Values may be sent and summed in bfloat16 or wider, within the bound.
No kernel may reach another device: no remote copies, remote signals or barrier semaphores. Data moves between devices by JAX's collectives and lax.ppermute only.
A program may use at most 128 MiB of HBM per device.

```python
import math
import jax
import jax.numpy as jnp
import numpy as np
from jax import lax

D = 6144
FF = 8192
TOP = 2
TOK_G = 128
EXPERTS = 4
CAP = 64
TOKENS = 512
N_EXPERT = 4
N_CUTS = 8


def with_spikes(values, key, source, target, blocks, factor):
    owner, partner = [(jnp.arange(values.shape[dim]) // (values.shape[dim] // blocks)).reshape([-1 if axis == dim else 1 for axis in range(values.ndim)]) for dim in (source, target)]
    chosen = jax.random.permutation(key, blocks)[partner]
    strong = (owner == chosen) | (owner == (partner + blocks // 2) % blocks)
    return jnp.where(strong, factor * values, values)


def shard_levels(rng, shape, cuts, low, high):
    def one(dim, parts):
        draws = jax.random.uniform(jax.random.fold_in(jax.random.fold_in(rng, 6), dim), (parts,), jnp.float32, low / len(cuts), high / len(cuts))
        return jnp.repeat(jnp.exp(draws), shape[dim] // parts).reshape((-1,) + (1,) * (len(shape) - dim - 1))

    gain = one(*cuts[0])
    for cut in cuts[1:]:
        gain = gain * one(*cut)
    return gain


def shared_out(key, own, number, rows, count, top, most, skew):
    order = jax.random.permutation(key, count)
    heavy_load, usual = load_shares(count, rows * top, most, skew, True), load_shares(count, rows * top, most, skew, False)
    places = jnp.arange(count)

    def named(lengths, turn):
        used = int((lengths > 0).sum())
        fixed = max(1, used // 4)
        passed = fixed + (places - fixed + turn * (used - fixed)) % max(1, count - fixed)
        return jnp.zeros((count,), jnp.int32).at[order[jnp.where(places < fixed, places, passed)]].set(jnp.asarray(lengths, jnp.int32))

    lengths = jnp.where(number % 4 == 0, named(heavy_load, number // 4), named(usual, number - number // 4 - 1))
    mixed = jax.random.permutation(jax.random.fold_in(own, 3), count)
    source_of, taker = mixed[0:count // 2 * 2:2], mixed[1:count // 2 * 2:2]
    room = jnp.minimum(lengths[source_of] - 1, most - lengths[taker]) // 2
    room = jnp.where((source_of == order[0]) | (taker == order[0]) | (lengths[taker] == 0), 0, jnp.maximum(room, 0))
    passed = jax.random.randint(jax.random.fold_in(own, 4), (count // 2,), 0, 1 << 20) % (room + 1)
    lengths = lengths.at[source_of].add(-passed).at[taker].add(passed)
    labels = jnp.searchsorted(jnp.cumsum(lengths), jnp.arange(rows * top), side="right").astype(jnp.int32)
    grid = labels.reshape(top, rows).T
    grid = grid[jax.random.permutation(jax.random.fold_in(own, 1), rows)]
    turn = jax.random.randint(jax.random.fold_in(own, 2), (rows, 1), 0, top)
    return jnp.take_along_axis(grid, (jnp.arange(top)[None, :] + turn) % top, axis=1)


def load_shares(number_of, total, bound, slope, full):
    weights = [(1 << 20) // math.isqrt(grade ** slope) + 1 for grade in range(1, number_of + 1)]
    largest = bound if full else min(bound, max(-(-total // number_of), total * weights[0] // sum(weights)))
    least = 1 if total - largest >= number_of - 1 else 0
    counts, surplus = [largest] + [least] * (number_of - 1), total - largest - least * (number_of - 1)
    while surplus > 0:
        movable = [i for i in range(1, number_of) if counts[i] < largest] or [i for i in range(1, number_of) if counts[i] < bound]
        mass, budget = sum([weights[i] for i in movable]), surplus
        for i in movable:
            more = min(bound - counts[i], max(1, budget * weights[i] // mass), surplus)
            counts[i] = counts[i] + more
            surplus = surplus - more
    return np.array(counts)


def scatter_about(stream_key, dims, deviation, reach, shards=(), kind=jnp.bfloat16):
    level = shard_levels(stream_key, dims, shards, -0.22, 0.18) if shards else 1.0
    result = jax.random.normal(stream_key, dims, jnp.float32) * deviation * level
    return jnp.minimum(jnp.maximum(result, -reach), reach).astype(kind)


def gaussian_with(rng, extent, deviation, limit, split, heavy, kind=jnp.bfloat16):
    entries = deviation * jax.random.normal(rng, extent, jnp.float32)
    if split:
        entries = entries * shard_levels(rng, extent, split, -0.22, 0.18)
    return jnp.clip(with_spikes(entries, jax.random.fold_in(rng, 3), *heavy), -limit, limit).astype(kind)


def setup_inputs(seed: int = 0) -> dict:
    key_of = jax.random.split(jax.random.key(seed), 9)
    out_grad = scatter_about(key_of[0], (TOKENS, D), 1.0, 6.0, ((0, 4), (1, 8)))
    gate_probs = jnp.clip(0.2 + 0.8 * jax.random.uniform(key_of[1], (TOKENS, TOP), jnp.float32) ** shard_levels(key_of[1], (TOKENS, TOP), ((0, 4),), -0.2, 0.2), 0.2, 1.0)
    expert_ids_keys = jax.random.split(jax.random.fold_in(key_of[2], 1), TOKENS // TOK_G)
    expert_ids_turns = jax.random.permutation(jax.random.fold_in(key_of[2], 3), TOKENS // TOK_G)
    expert_ids = jax.vmap(lambda own, number: shared_out(jax.random.fold_in(key_of[2], 2), own, number, TOK_G, EXPERTS, TOP, CAP, 2))(expert_ids_keys, expert_ids_turns).reshape((TOKENS, TOP))
    gate_pre = scatter_about(key_of[3], (EXPERTS, N_EXPERT, CAP, FF), 1.0, 6.0, ((0, 4), (3, 8)))
    up_pre = scatter_about(key_of[4], (EXPERTS, N_EXPERT, CAP, FF), 1.0, 6.0, ((0, 4), (3, 8)))
    w_gate = gaussian_with(key_of[5], (EXPERTS, D, FF), D ** -0.5, 0.109375, ((0, 4), (2, 8)), (2, 1, 8, 2.0))
    w_up = gaussian_with(key_of[6], (EXPERTS, D, FF), D ** -0.5, 0.109375, ((0, 4), (2, 8)), (2, 1, 8, 2.0))
    w_down = scatter_about(key_of[7], (EXPERTS, FF, D), FF ** -0.5, 0.0625, ((0, 4), (1, 8)))
    return {"out_grad": out_grad, "gate_probs": gate_probs, "expert_ids": expert_ids, "gate_pre": gate_pre, "up_pre": up_pre, "w_gate": w_gate, "w_up": w_up, "w_down": w_down}


def slot_tables(routing):
    chosen = routing.reshape(-1).astype(jnp.int32)
    onehot = (chosen[:, None] == jnp.arange(EXPERTS, dtype=jnp.int32)[None, :]).astype(jnp.int32)
    earlier = jnp.cumsum(onehot, axis=0) - onehot
    position = jnp.sum(earlier * onehot, axis=1)
    target = (chosen * CAP + position).astype(jnp.int32)
    source = jnp.full((EXPERTS * CAP,), chosen.shape[0], jnp.int32)
    source = source.at[target].set(jnp.arange(chosen.shape[0], dtype=jnp.int32))
    return target, source


def pack_group(inputs):
    out_rows, gate_values, routing = inputs
    target, source = slot_tables(routing)
    weighted = (gate_values[:, :, None] * out_rows[:, None, :].astype(jnp.float32)).astype(jnp.bfloat16)
    weighted = weighted.reshape(TOK_G * TOP, D)
    weighted = jnp.concatenate([weighted, jnp.zeros((1, D), jnp.bfloat16)], axis=0)
    return jnp.take(weighted, source, axis=0).reshape(EXPERTS, CAP, D)


def expert_backward(inputs):
    routed, gate_saved, up_saved, gate_weight, up_weight, down_weight = inputs
    hidden_grad = jnp.dot(routed, down_weight.T, preferred_element_type=jnp.float32)
    gate_act = gate_saved.reshape(-1, FF).astype(jnp.float32)
    up_act = up_saved.reshape(-1, FF).astype(jnp.float32)
    logistic = jax.nn.sigmoid(gate_act)
    up_grad = (hidden_grad * gate_act * logistic).astype(jnp.bfloat16)
    gate_grad = (hidden_grad * up_act * logistic * (1.0 + gate_act * (1.0 - logistic))).astype(jnp.bfloat16)
    hidden_act = (gate_act * logistic * up_act).astype(jnp.bfloat16)
    down_grad = jnp.dot(hidden_act.T, routed, preferred_element_type=jnp.float32).astype(jnp.bfloat16)
    block_width = FF // N_CUTS

    def add_block(running, block_index):
        first_unit = (block_index * block_width).astype(jnp.int32)
        gate_part = lax.dynamic_slice_in_dim(gate_grad, first_unit, block_width, 1)
        up_part = lax.dynamic_slice_in_dim(up_grad, first_unit, block_width, 1)
        gate_cols = lax.dynamic_slice_in_dim(gate_weight, first_unit, block_width, 1)
        up_cols = lax.dynamic_slice_in_dim(up_weight, first_unit, block_width, 1)
        partial_value = jnp.dot(gate_part, gate_cols.T, preferred_element_type=jnp.float32)
        partial_value = partial_value + jnp.dot(up_part, up_cols.T, preferred_element_type=jnp.float32)
        rounded = lax.optimization_barrier(partial_value.astype(jnp.bfloat16)).astype(jnp.float32)
        return running + rounded, None

    running, unused = lax.scan(add_block, jnp.zeros((routed.shape[0], D), jnp.float32),
                               jnp.arange(N_CUTS, dtype=jnp.int32))
    return running, down_grad


def reference(out_grad, gate_probs, expert_ids, gate_pre, up_pre, w_gate, w_up, w_down):
    grouped = out_grad.reshape(N_EXPERT, TOK_G, D)
    probs_grouped = gate_probs.reshape(N_EXPERT, TOK_G, TOP)
    ids_grouped = expert_ids.reshape(N_EXPERT, TOK_G, TOP)
    packed = lax.map(pack_group, (grouped, probs_grouped, ids_grouped))
    routed = jnp.transpose(packed, (1, 0, 2, 3)).reshape(EXPERTS, N_EXPERT * CAP, D)
    summed, w_down_grad = lax.map(expert_backward, (routed, gate_pre, up_pre, w_gate, w_up, w_down))
    by_group = jnp.transpose(summed.reshape(EXPERTS, N_EXPERT, CAP, D), (1, 0, 2, 3))
    by_group = by_group.reshape(N_EXPERT, EXPERTS * CAP, D)

    def combine(inputs):
        sums_here, routing = inputs
        target, source = slot_tables(routing)
        picked = jnp.take(sums_here, target, axis=0).reshape(TOK_G, TOP, D)
        return jnp.sum(picked, axis=1).astype(jnp.bfloat16)

    input_grad = lax.map(combine, (by_group, ids_grouped)).reshape(N_EXPERT * TOK_G, D)
    return input_grad, w_down_grad
```

```python
import functools
import jax
import jax.numpy as jnp
from jax import lax
from jax.experimental import pallas as pl
from jax.experimental.pallas import tpu as pltpu
from jax.sharding import PartitionSpec as P

BF16 = jnp.bfloat16
F32 = jnp.float32
VMEM = pl.BlockSpec(memory_space=pltpu.VMEM)
SMEM = pl.BlockSpec(memory_space=pltpu.SMEM)
NT = (((1,), (1,)), ((), ()))
TN = (((0,), (0,)), ((), ()))
NN = (((1,), (0,)), ((), ()))
MIB = 1 << 20


def dot(a, b, dims):
    return lax.dot_general(a, b, dims, preferred_element_type=F32)


def cost(flops, bytes_accessed):
    return pl.CostEstimate(flops=int(flops), bytes_accessed=int(bytes_accessed), transcendentals=0)


def params(mib, axes=0):
    return pltpu.CompilerParams(
        vmem_limit_bytes=mib * MIB,
        dimension_semantics=("arbitrary",) * axes if axes else None,
    )


def route(where, ids, probs, experts, capacity):
    tokens = ids.shape[1]
    lines = max(8, experts)
    rows = experts * capacity

    def kernel(where_ref, ids_ref, probs_ref, sel_ref, gate_ref):
        me = where_ref[0]
        expert = lax.broadcasted_iota(jnp.int32, (lines, tokens), 0) ^ me
        first = (ids_ref[0:1, :] == expert).astype(F32)
        second = (ids_ref[1:2, :] == expert).astype(F32)
        hit = first + second
        before = lax.broadcasted_iota(jnp.int32, (tokens, tokens), 0)
        after = lax.broadcasted_iota(jnp.int32, (tokens, tokens), 1)
        earlier = (before < after).astype(F32).astype(BF16)
        place = dot(hit.astype(BF16), earlier, NN)
        place = jnp.where(hit > 0.0, place, -1.0)
        gate = first * probs_ref[0:1, :] + second * probs_ref[1:2, :]
        slot = lax.broadcasted_iota(jnp.int32, (capacity, tokens), 0).astype(F32)
        for r in range(experts):
            match = place[r : r + 1, :] == slot
            span = pl.ds(r * capacity, capacity)
            sel_ref[span, :] = jnp.where(match, 1.0, 0.0).astype(BF16)
            gate_ref[span, :] = jnp.sum(
                jnp.where(match, gate[r : r + 1, :], 0.0), axis=1, keepdims=True
            )

    return pl.pallas_call(
        kernel,
        out_shape=(
            jax.ShapeDtypeStruct((rows, tokens), BF16),
            jax.ShapeDtypeStruct((rows, 1), F32),
        ),
        in_specs=[SMEM, VMEM, VMEM],
        out_specs=(VMEM, VMEM),
        cost_estimate=cost(1e6, 2e5),
        name="route",
    )(where, ids, probs)


def pack(raws, sel, gate, experts, capacity):
    blocks = len(raws)
    columns = raws[0].shape[1]

    def kernel(*refs):
        raw_refs, (sel_ref, gate_ref), out_refs = (
            refs[:blocks],
            refs[blocks : blocks + 2],
            refs[blocks + 2 :],
        )
        for b in range(blocks):
            rows = (dot(sel_ref[...], raw_refs[b][...], NN) * gate_ref[...]).astype(BF16)
            for r in range(experts):
                out_refs[r][b] = rows[r * capacity : (r + 1) * capacity]

    return pl.pallas_call(
        kernel,
        out_shape=[jax.ShapeDtypeStruct((blocks, capacity, columns), BF16)] * experts,
        in_specs=[VMEM] * (blocks + 2),
        out_specs=[VMEM] * experts,
        compiler_params=params(32),
        cost_estimate=cost(
            2 * blocks * sel.shape[0] * sel.shape[1] * columns, 4e5 * blocks
        ),
        name="pack",
    )(*raws, sel, gate)


def activations(where, gate_pre, up_pre):
    _, groups, capacity, units = gate_pre.shape
    rows = groups * capacity
    tile = 256

    def kernel(where_ref, gate_ref, up_ref, up_factor, gate_factor, act):
        me = where_ref[0]
        for r in range(groups):
            a = gate_ref[0, me ^ r].astype(F32)
            b = up_ref[0, me ^ r].astype(F32)
            sig = 1.0 / (1.0 + jnp.exp(-a))
            span = pl.ds(r * capacity, capacity)
            swish = a * sig
            up_factor[span, :] = swish
            gate_factor[span, :] = b * sig * (1.0 + a * (1.0 - sig))
            act[span, :] = (swish * b).astype(BF16)

    spec = pl.BlockSpec((1, groups, capacity, tile), lambda i, w: (0, 0, 0, i))
    out = pl.BlockSpec((rows, tile), lambda i, w: (0, i))
    return pl.pallas_call(
        kernel,
        out_shape=(
            jax.ShapeDtypeStruct((rows, units), F32),
            jax.ShapeDtypeStruct((rows, units), F32),
            jax.ShapeDtypeStruct((rows, units), BF16),
        ),
        grid_spec=pltpu.PrefetchScalarGridSpec(
            num_scalar_prefetch=1,
            grid=(units // tile,),
            in_specs=[spec, spec],
            out_specs=(out, out, out),
        ),
        compiler_params=params(24, 1),
        cost_estimate=cost(1e7, 14 * rows * units),
        name="activations",
    )(where, gate_pre, up_pre)


def block_of(where, shift, line, sibling):
    cut = where[1]
    z = lax.rem(lax.div(cut, 2) + (shift + line), line)
    core = lax.rem(cut, 2)
    return z * 2 + (1 - core if sibling else core)


def pick(step, values):
    result = jnp.int32(values[0])
    for i, value in enumerate(values[1:], 1):
        result = jnp.where(step == i, jnp.int32(value), result)
    return result


def hidden_part(where, x, w_down, shifts, line, sibling, total, factors):
    blocks, rows, columns = x.shape
    units = w_down.shape[1]
    tile = 256
    tiles = units // tile
    has_total = total is not None
    last = factors is not None

    def kernel(where_ref, *refs):
        refs = list(refs)
        x_ref, w_ref = refs.pop(0), refs.pop(0)
        total_ref = refs.pop(0) if has_total else None
        factor_refs = (refs.pop(0), refs.pop(0)) if last else None
        b, i = pl.program_id(0), pl.program_id(1)
        acc = refs[-1]
        span = pl.ds(pl.multiple_of(i * tile, tile), tile)
        value = dot(x_ref[0], w_ref[0], NT)

        def finish(value):
            if not last:
                acc[:, span] = value
                return
            if blocks > 1:
                acc[:, span] = value

            @pl.when(b == blocks - 1)
            def _():
                refs[0][:, span] = (value * factor_refs[0][:, span]).astype(BF16)
                refs[1][:, span] = (value * factor_refs[1][:, span]).astype(BF16)

        @pl.when(b == 0)
        def _():
            finish(value + total_ref[:, span] if has_total else value)

        if blocks > 1:

            @pl.when(b > 0)
            def _():
                finish(acc[:, span] + value)

    whole = pl.BlockSpec((rows, units), lambda b, i, w: (0, 0))
    in_specs = [
        pl.BlockSpec((1, rows, columns), lambda b, i, w: (b, 0, 0)),
        pl.BlockSpec(
            (1, tile, columns),
            lambda b, i, w: (0, i, block_of(w, pick(b, [-s for s in shifts]), line, sibling)),
        ),
    ]
    operands = [x, w_down]
    if has_total:
        in_specs.append(whole)
        operands.append(total)
    scratch = []
    if last:
        in_specs += [whole, whole]
        operands += list(factors)
        out_shape = [jax.ShapeDtypeStruct((rows, units), BF16)] * 2
        out_specs = [whole, whole]
        scratch = [pltpu.VMEM((rows, units), F32)]
    else:
        out_shape = jax.ShapeDtypeStruct((rows, units), F32)
        out_specs = whole
    return pl.pallas_call(
        kernel,
        out_shape=out_shape,
        grid_spec=pltpu.PrefetchScalarGridSpec(
            num_scalar_prefetch=1,
            grid=(blocks, tiles),
            in_specs=in_specs,
            out_specs=out_specs,
            scratch_shapes=scratch,
        ),
        compiler_params=params(32, 2),
        cost_estimate=cost(
            2 * blocks * rows * columns * units, 2 * blocks * columns * units + 8 * rows * units
        ),
        name="hidden_part",
    )(where, *operands)


def down_part(where, act, mine, theirs, shifts, line, before, out_shape):
    blocks, rows, columns = mine.shape
    units = act.shape[1]

    def kernel(where_ref, act_ref, mine_ref, theirs_ref, *refs):
        out_ref = refs[-1]
        i = pl.program_id(0)

        @pl.when(i < blocks)
        def _():
            out_ref[0] = dot(act_ref[...], mine_ref[0], TN).astype(BF16)

        @pl.when(i >= blocks)
        def _():
            out_ref[0] = dot(act_ref[...], theirs_ref[0], TN).astype(BF16)

    def out_map(i, w):
        shift = pick(lax.rem(i, blocks), [-s for s in shifts])
        own = block_of(w, shift, line, False)
        other = block_of(w, shift, line, True)
        return (0, 0, jnp.where(i < blocks, own, other))

    in_specs = [
        pl.BlockSpec((rows, units), lambda i, w: (0, 0)),
        pl.BlockSpec((1, rows, columns), lambda i, w: (jnp.minimum(i, blocks - 1), 0, 0)),
        pl.BlockSpec((1, rows, columns), lambda i, w: (jnp.maximum(i - blocks, 0), 0, 0)),
    ]
    operands = [act, mine, theirs]
    if before is not None:
        in_specs.append(pl.BlockSpec(memory_space=pl.ANY))
        operands.append(before)
    return pl.pallas_call(
        kernel,
        out_shape=jax.ShapeDtypeStruct(out_shape, BF16),
        grid_spec=pltpu.PrefetchScalarGridSpec(
            num_scalar_prefetch=1,
            grid=(2 * blocks,),
            in_specs=in_specs,
            out_specs=pl.BlockSpec((1, units, columns), out_map),
        ),
        input_output_aliases={} if before is None else {4: 0},
        compiler_params=params(24, 1),
        cost_estimate=cost(4 * blocks * rows * columns * units, 4 * blocks * columns * units),
        name="down_part",
    )(where, *operands)


def slot_part(where, gate_grad, up_grad, w_gate, w_up, shifts, line, sibling, arrived, experts):
    rows, units = gate_grad.shape
    blocks = len(shifts)
    columns = w_gate.shape[1] // (2 * line)
    tile = 256
    capacity = rows // experts

    def kernel(where_ref, gate_ref, up_ref, wg_ref, wu_ref, *refs):
        value = dot(gate_ref[...], wg_ref[0], NT) + dot(up_ref[...], wu_ref[0], NT)
        if arrived is None:
            refs[0][0] = value.astype(BF16)
        else:
            value = (value + refs[0][0].astype(F32)).astype(BF16)
            for r in range(experts):
                refs[1 + r][0] = value[r * capacity : (r + 1) * capacity]

    tiles = columns // tile
    whole = pl.BlockSpec((rows, units), lambda b, i, w: (0, 0))
    weight = pl.BlockSpec(
        (1, tile, units),
        lambda b, i, w: (0, block_of(w, pick(b, shifts), line, sibling) * tiles + i, 0),
    )
    part = pl.BlockSpec((1, rows, tile), lambda b, i, w: (b, 0, i))
    in_specs = [whole, whole, weight, weight]
    operands = [gate_grad, up_grad, w_gate, w_up]
    if arrived is None:
        out_shape = jax.ShapeDtypeStruct((blocks, rows, columns), BF16)
        out_specs = part
    else:
        in_specs.append(part)
        operands.append(arrived)
        out_shape = [jax.ShapeDtypeStruct((blocks, capacity, columns), BF16)] * experts
        out_specs = [pl.BlockSpec((1, capacity, tile), lambda b, i, w: (b, 0, i))] * experts
    return pl.pallas_call(
        kernel,
        out_shape=out_shape,
        grid_spec=pltpu.PrefetchScalarGridSpec(
            num_scalar_prefetch=1, grid=(blocks, tiles), in_specs=in_specs, out_specs=out_specs
        ),
        compiler_params=params(24, 2),
        cost_estimate=cost(
            4 * blocks * rows * columns * units, 4 * blocks * columns * units + 4 * rows * units
        ),
        name="slot_part",
    )(where, *operands)


def combine(pieces, sel, others):
    experts = len(pieces)
    blocks, capacity, columns = pieces[0].shape
    tokens = sel.shape[1]
    count = len(others)

    def kernel(*refs):
        piece_refs, sel_ref = refs[:experts], refs[experts]
        other_refs = refs[experts + 1 : experts + 1 + count]
        out_refs = refs[experts + 1 + count :]
        for b in range(blocks):
            rows = jnp.concatenate([piece[b] for piece in piece_refs], axis=0)
            value = dot(sel_ref[...], rows, TN)
            for other in other_refs:
                value = value + other[...].astype(F32)
            out_refs[b][...] = value.astype(BF16)

    return pl.pallas_call(
        kernel,
        out_shape=[jax.ShapeDtypeStruct((tokens, columns), BF16)] * blocks,
        in_specs=[VMEM] * (experts + 1 + count),
        out_specs=[VMEM] * blocks,
        compiler_params=params(32),
        cost_estimate=cost(
            2 * blocks * experts * capacity * tokens * columns, 6e5 * blocks + 2e5 * count
        ),
        name="combine",
    )(*pieces, sel, *others)


def slot_tables(routing, experts, capacity):
    chosen = routing.reshape(-1)
    onehot = (chosen[:, None] == jnp.arange(experts, dtype=jnp.int32)[None, :]).astype(jnp.int32)
    earlier = jnp.cumsum(onehot, axis=0) - onehot
    position = jnp.sum(earlier * onehot, axis=1)
    target = chosen * capacity + position
    source = jnp.full((experts * capacity,), chosen.shape[0], jnp.int32)
    source = source.at[target].set(jnp.arange(chosen.shape[0], dtype=jnp.int32))
    return (target, source)


def pack_rows(out_rows, gate_values, source, experts, capacity):
    columns = out_rows.shape[1]
    weighted = (gate_values[:, :, None] * out_rows[:, None, :].astype(jnp.float32)).astype(
        jnp.bfloat16
    )
    weighted = weighted.reshape(-1, columns)
    weighted = jnp.concatenate([weighted, jnp.zeros((1, columns), jnp.bfloat16)], axis=0)
    return jnp.take(weighted, source, axis=0).reshape(experts, capacity, columns)


def on_any_tiling(out_grad, gate_probs, expert_ids, gate_pre, up_pre, w_gate, w_up, w_down):
    tokens_here = expert_ids.shape[0]
    experts = lax.axis_size("expert") * w_gate.shape[0]
    groups = gate_pre.shape[1]
    capacity = gate_pre.shape[2]
    units = gate_pre.shape[3]
    local_cols = out_grad.shape[1]
    slot_rows = groups * capacity
    target, source = slot_tables(expert_ids, experts, capacity)
    down_weight = w_down[0]
    contract_last = (((1,), (1,)), ((), ()))
    contract_first = (((0,), (0,)), ((), ()))
    gate_act = gate_pre[0].reshape(slot_rows, units).astype(jnp.float32)
    up_act = up_pre[0].reshape(slot_rows, units).astype(jnp.float32)
    logistic = jax.nn.sigmoid(gate_act)
    hidden_act = (gate_act * logistic * up_act).astype(jnp.bfloat16)
    features = lax.all_gather(out_grad, "cuts", axis=1, tiled=True)
    outgoing = pack_rows(features, gate_probs, source, experts, capacity)
    routed = lax.all_to_all(outgoing, "expert", split_axis=0, concat_axis=0, tiled=True)
    routed = routed.reshape(slot_rows, routed.shape[2])
    hidden_grad = lax.dot_general(
        routed, down_weight, contract_last, preferred_element_type=jnp.float32
    )
    down_grad = lax.dot_general(
        hidden_act, routed, contract_first, preferred_element_type=jnp.float32
    )
    w_down_grad = down_grad.astype(jnp.bfloat16)[None]
    up_grad = (hidden_grad * gate_act * logistic).astype(jnp.bfloat16)
    gate_grad = (hidden_grad * up_act * logistic * (1.0 + gate_act * (1.0 - logistic))).astype(
        jnp.bfloat16
    )
    gate_weight = w_gate[0]
    up_weight = w_up[0]
    partial_value = lax.dot_general(
        gate_weight, gate_grad, contract_last, preferred_element_type=jnp.float32
    )
    partial_value = partial_value + lax.dot_general(
        up_weight, up_grad, contract_last, preferred_element_type=jnp.float32
    )
    summed = lax.psum_scatter(
        lax.optimization_barrier(partial_value.astype(jnp.bfloat16))
        .astype(jnp.float32)
        .astype(jnp.bfloat16),
        "cuts",
        scatter_dimension=0,
        tiled=True,
    ).astype(jnp.float32)
    summed = summed.reshape(local_cols, groups, capacity)
    returned = lax.all_to_all(
        summed.astype(jnp.bfloat16), "expert", split_axis=1, concat_axis=1, tiled=True
    ).astype(summed.dtype)
    flat_back = returned.reshape(local_cols, experts * capacity)
    picked = jnp.take(flat_back, target, axis=1).reshape(local_cols, tokens_here, -1)
    input_grad = jnp.sum(picked, axis=2)
    return (input_grad.T.astype(jnp.bfloat16), w_down_grad)


def on_device(out_grad, gate_probs, expert_ids, gate_pre, up_pre, w_gate, w_up, w_down):
    experts = lax.axis_size("expert")
    cuts = lax.axis_size("cuts")
    line = cuts // 2
    capacity = gate_pre.shape[2]
    if out_grad.shape[1] % 256 or gate_pre.shape[3] % 256 or capacity % 16 or cuts % 2:
        return on_any_tiling(
            out_grad, gate_probs, expert_ids, gate_pre, up_pre, w_gate, w_up, w_down
        )
    where = jnp.stack([lax.axis_index("expert"), lax.axis_index("cuts")]).astype(jnp.int32)
    groups = [g for g in ([0], sorted({1, line - 1}), list(range(2, line - 1))) if g]

    def along(x, shift):
        pairs = [(i, (i + 2 * shift) % cuts) for i in range(cuts)]
        return lax.ppermute(x, "cuts", pairs)

    def swap(x):
        return lax.ppermute(x, "cuts", [(i, i ^ 1) for i in range(cuts)])

    def exchange(pieces):
        moved = [
            lax.ppermute(pieces[r], "expert", [(i, i ^ r) for i in range(experts)])
            for r in range(1, experts)
        ]
        return [pieces[0]] + moved

    sel, gate = route(where, expert_ids.T, gate_probs.T, experts, capacity)
    up_factor, gate_factor, act = activations(where, gate_pre, up_pre)
    total = None
    routed = []
    for group in groups:
        raws = [along(out_grad, shift) if shift else out_grad for shift in group]
        pieces = exchange(pack(raws, sel, gate, experts, capacity))
        mine = jnp.concatenate(pieces, axis=1)
        theirs = swap(mine)
        routed.append((mine, theirs))
        total = hidden_part(where, mine, w_down, group, line, False, total, None)
        last = group is groups[-1]
        total = hidden_part(
            where, theirs, w_down, group, line, True, total,
            (gate_factor, up_factor) if last else None,
        )
    gate_grad, up_grad = total

    order = groups[::-1]
    back = functools.partial(slot_part, where, gate_grad, up_grad, w_gate, w_up)
    arrived = [swap(back(group, line, True, None, experts)) for group in order]
    landed = []
    result = None
    for group, other in zip(order, arrived):
        pieces = exchange(back(group, line, False, other, experts))
        if group != [0]:
            for shift, part in zip(group, combine(pieces, sel, [])):
                landed.append(along(part, shift))
        else:
            result = combine(pieces, sel, landed)[0]
    down = None
    for group, (mine, theirs) in zip(groups, routed):
        down = down_part(where, act, mine, theirs, group, line, down, w_down.shape)
    return result, down


def solution(mesh):
    return jax.shard_map(
        on_device,
        mesh=mesh,
        in_specs=(
            P("expert", "cuts"),
            P("expert", None),
            P("expert", None),
            P("expert", None, None, "cuts"),
            P("expert", None, None, "cuts"),
            P("expert", None, "cuts"),
            P("expert", None, "cuts"),
            P("expert", "cuts", None),
        ),
        out_specs=(P("expert", "cuts"), P("expert", "cuts", None)),
        check_vma=False,
    )
```

```python
import functools
import jax
import jax.numpy as jnp
from jax import lax
from jax.experimental import pallas as pl
from jax.experimental.pallas import tpu as pltpu
from jax.sharding import PartitionSpec as P

BF16 = jnp.bfloat16
F32 = jnp.float32
VMEM = pl.BlockSpec(memory_space=pltpu.VMEM)
ANY = pl.BlockSpec(memory_space=pl.ANY)
NT = (((1,), (1,)), ((), ()))
TN = (((0,), (0,)), ((), ()))
NN = (((1,), (0,)), ((), ()))
MIB = 1 << 20


def dot(a, b, dims):
    return lax.dot_general(a, b, dims, preferred_element_type=F32)


def shaped(shape, dtype):
    return jax.ShapeDtypeStruct(shape, dtype)


def call(kernel, name, operands, out_shape, after=(), flops=0, moved=0, mib=8, out_specs=None, **more):
    count, extra, results = len(operands), len(after), len(out_shape)

    def body(*refs):
        outs = refs[count + extra :]
        kernel(*refs[:count], *outs[:results], *outs[results + 1 :])
        outs[results][...] = jnp.zeros((8, 128), F32)

    out_shape = list(out_shape) + [shaped((8, 128), F32)]
    out_specs = list(out_specs or [VMEM] * results) + [VMEM]
    specs = more.pop("in_specs", [VMEM] * count)
    return pl.pallas_call(
        body,
        out_shape=out_shape,
        in_specs=list(specs) + [VMEM] * extra,
        out_specs=out_specs,
        compiler_params=pltpu.CompilerParams(vmem_limit_bytes=mib * MIB),
        cost_estimate=pl.CostEstimate(
            flops=int(flops), bytes_accessed=int(moved), transcendentals=0
        ),
        name=name,
        **more,
    )(*operands, *after)


def fill(raw, sel, gate, outs, b, capacity):
    rows = (dot(sel, raw, NN) * gate).astype(BF16)
    for r, out in enumerate(outs):
        out[b] = rows[r * capacity : (r + 1) * capacity]


def first_pack(raw, ids, probs, experts, capacity):
    tokens, columns = raw.shape
    lines = max(8, experts)
    rows = experts * capacity

    def kernel(raw_ref, ids_ref, probs_ref, sel_ref, gate_ref, copy_ref, *outs):
        copy_ref[...] = raw_ref[...]
        me = lax.axis_index("expert")
        expert = lax.broadcasted_iota(jnp.int32, (lines, tokens), 0) ^ me
        first = (ids_ref[0:1, :] == expert).astype(F32)
        second = (ids_ref[1:2, :] == expert).astype(F32)
        hit = first + second
        before = lax.broadcasted_iota(jnp.int32, (tokens, tokens), 0)
        here = lax.broadcasted_iota(jnp.int32, (tokens, tokens), 1)
        earlier = (before < here).astype(F32).astype(BF16)
        place = dot(hit.astype(BF16), earlier, NN)
        place = jnp.where(hit > 0.0, place, -1.0)
        gate = first * probs_ref[0:1, :] + second * probs_ref[1:2, :]
        slot = lax.broadcasted_iota(jnp.int32, (capacity, tokens), 0).astype(F32)
        for r in range(experts):
            match = place[r : r + 1, :] == slot
            span = pl.ds(r * capacity, capacity)
            sel_ref[span, :] = jnp.where(match, 1.0, 0.0).astype(BF16)
            gate_ref[span, :] = jnp.sum(
                jnp.where(match, gate[r : r + 1, :], 0.0), axis=1, keepdims=True
            )
        fill(raw_ref[...], sel_ref[...], gate_ref[...], outs, 0, capacity)

    return call(
        kernel,
        "first_pack",
        [raw, ids, probs],
        [shaped((rows, tokens), BF16), shaped((rows, 1), F32), shaped(raw.shape, BF16)]
        + [shaped((1, capacity, columns), BF16)] * experts,
        flops=2 * rows * tokens * columns,
        moved=1e6,
    )


def pack(raws, sel, gate, experts, capacity, after):
    blocks = len(raws)
    columns = raws[0].shape[1]

    def kernel(*refs):
        sel_ref, gate_ref = refs[blocks : blocks + 2]
        for b in range(blocks):
            fill(refs[b][...], sel_ref[...], gate_ref[...], refs[blocks + 2 :], b, capacity)

    return call(
        kernel,
        "pack",
        [*raws, sel, gate],
        [shaped((blocks, capacity, columns), BF16)] * experts,
        after,
        flops=2 * blocks * sel.shape[0] * sel.shape[1] * columns,
        moved=6e5 * blocks,
    )


def activations(gate_pre, up_pre, after):
    _, groups, capacity, units = gate_pre.shape
    rows = groups * capacity

    def kernel(gate_ref, up_ref, up_factor, gate_factor, act):
        me = lax.axis_index("expert")
        tile = 256

        def step(i, unused):
            span = pl.ds(pl.multiple_of(i * tile, tile), tile)
            a = jnp.concatenate([gate_ref[0, me ^ r, :, span] for r in range(groups)], axis=0)
            b = jnp.concatenate([up_ref[0, me ^ r, :, span] for r in range(groups)], axis=0)
            a = a.astype(F32).T
            b = b.astype(F32).T
            sig = 1.0 / (1.0 + jnp.exp(-a))
            swish = a * sig
            up_factor[span, :] = swish
            gate_factor[span, :] = b * sig * (1.0 + a * (1.0 - sig))
            act[span, :] = (swish * b).astype(BF16)
            return unused

        lax.fori_loop(0, units // tile, step, 0)

    return call(
        kernel,
        "activations",
        [gate_pre, up_pre],
        [shaped((units, rows), F32), shaped((units, rows), F32), shaped((units, rows), BF16)],
        after,
        flops=3e7,
        moved=14 * rows * units,
    )


def block_of(shift, line, sibling):
    cut = lax.axis_index("cuts")
    z = lax.rem(lax.div(cut, 2) + (shift + line), line)
    core = lax.rem(cut, 2)
    return z * 2 + (1 - core if sibling else core)


def hidden_part(x, w_down, shifts, line, sibling, total, factors, after):
    blocks, rows, columns = x.shape
    units = w_down.shape[1]
    tile = 256
    has_total = total is not None

    def kernel(x_ref, w_ref, *refs):
        outs = refs[has_total + len(factors) :]
        factor_refs = refs[has_total : has_total + len(factors)]
        starts = [
            pl.multiple_of(block_of(-s, line, sibling) * columns, 128) for s in shifts
        ]

        def step(i, unused):
            span = pl.ds(pl.multiple_of(i * tile, tile), tile)
            value = refs[0][span, :] if has_total else 0.0
            for b, start in enumerate(starts):
                value = value + dot(w_ref[0, span, pl.ds(start, columns)], x_ref[b], NT)
            if factors:
                for out, factor in zip(outs, factor_refs):
                    out[span, :] = (value * factor[span, :]).astype(BF16)
            else:
                outs[0][span, :] = value
            return unused

        lax.fori_loop(0, units // tile, step, 0)

    return call(
        kernel,
        "hidden_part",
        [x, w_down] + ([total] if has_total else []) + list(factors),
        [shaped((units, rows), BF16)] * 2 if factors else [shaped((units, rows), F32)],
        after,
        flops=2 * blocks * rows * columns * units,
        moved=2 * blocks * columns * units + 8 * rows * units,
    )


def down_part(act, mine, theirs, shifts, line, before, out_shape, after):
    blocks, rows, columns = mine.shape
    units = act.shape[0]
    split = 4
    part = units // split
    steps = [(half, b) for half in range(2) for b in range(blocks)]

    def kernel(act_ref, mine_ref, theirs_ref, *refs):
        out_ref, held, sems = refs[-3:]
        copies = []
        for i, (half, b) in enumerate(steps):
            start = pl.multiple_of(block_of(-shifts[b], line, bool(half)) * columns, 128)
            now = i % 2
            x = (theirs_ref if half else mine_ref)[b]
            for j in range(split):
                if i >= 2:
                    copies[(i - 2) * split + j].wait()
                span = pl.ds(j * part, part)
                held[now, span, :] = dot(act_ref[span, :], x, NN).astype(BF16)
                copy = pltpu.make_async_copy(
                    held.at[now, span, :],
                    out_ref.at[0, span, pl.ds(start, columns)],
                    sems.at[now, j],
                )
                copy.start()
                copies.append(copy)
        for copy in copies[-2 * split :]:
            copy.wait()

    operands = [act, mine, theirs]
    if before is not None:
        operands.append(before)
    return call(
        kernel,
        "down_part",
        operands,
        [shaped(out_shape, BF16)],
        after,
        flops=4 * blocks * rows * columns * units,
        moved=4 * blocks * columns * units,
        in_specs=[VMEM] * 3 + [ANY] * (len(operands) - 3),
        out_specs=[ANY],
        input_output_aliases={} if before is None else {3: 0},
        scratch_shapes=[
            pltpu.VMEM((2, units, columns), BF16),
            pltpu.SemaphoreType.DMA((2, split)),
        ],
    )


def slot_part(gate_grad, up_grad, w_gate, w_up, shifts, line, sibling, arrived, experts, after):
    units, rows = gate_grad.shape
    blocks = len(shifts)
    columns = w_gate.shape[1] // (2 * line)
    tile = 256
    capacity = rows // experts
    split = arrived is not None

    def kernel(gate_ref, up_ref, wg_ref, wu_ref, *refs):
        for b, shift in enumerate(shifts):
            base = block_of(shift, line, sibling) * columns
            for i in range(columns // tile):
                span = pl.ds(pl.multiple_of(base + i * tile, tile), tile)
                value = dot(wg_ref[0, span, :], gate_ref[...], NN)
                value = (value + dot(wu_ref[0, span, :], up_ref[...], NN)).T
                out = pl.ds(i * tile, tile)
                if not split:
                    refs[0][b, :, out] = value.astype(BF16)
                    continue
                value = (value + refs[0][b, :, out].astype(F32)).astype(BF16)
                for r in range(experts):
                    refs[1 + r][b, :, out] = value[r * capacity : (r + 1) * capacity]

    if split:
        out_shape = [shaped((blocks, capacity, columns), BF16)] * experts
    else:
        out_shape = [shaped((blocks, rows, columns), BF16)]
    return call(
        kernel,
        "slot_part",
        [gate_grad, up_grad, w_gate, w_up] + ([arrived] if split else []),
        out_shape,
        after,
        flops=4 * blocks * rows * columns * units,
        moved=4 * blocks * columns * units + 4 * rows * units,
    )


def combine(pieces, sel, others, after):
    experts = len(pieces)
    blocks, _, columns = pieces[0].shape
    tokens = sel.shape[1]
    count = len(others)

    def kernel(*refs):
        piece_refs, sel_ref = refs[:experts], refs[experts]
        other_refs = refs[experts + 1 : experts + 1 + count]
        out_refs = refs[experts + 1 + count :]
        for b in range(blocks):
            rows = jnp.concatenate([piece[b] for piece in piece_refs], axis=0)
            value = dot(sel_ref[...], rows, TN)
            for other in other_refs:
                value = value + other[...].astype(F32)
            out_refs[b][...] = value.astype(BF16)

    return call(
        kernel,
        "combine",
        [*pieces, sel, *others],
        [shaped((tokens, columns), BF16)] * blocks,
        after,
        flops=2 * blocks * sel.shape[0] * tokens * columns,
        moved=6e5 * blocks + 2e5 * count,
    )


def slot_tables(routing, experts, capacity):
    chosen = routing.reshape(-1)
    onehot = (chosen[:, None] == jnp.arange(experts, dtype=jnp.int32)[None, :]).astype(jnp.int32)
    earlier = jnp.cumsum(onehot, axis=0) - onehot
    position = jnp.sum(earlier * onehot, axis=1)
    target = chosen * capacity + position
    source = jnp.full((experts * capacity,), chosen.shape[0], jnp.int32)
    source = source.at[target].set(jnp.arange(chosen.shape[0], dtype=jnp.int32))
    return (target, source)


def pack_rows(out_rows, gate_values, source, experts, capacity):
    columns = out_rows.shape[1]
    weighted = (gate_values[:, :, None] * out_rows[:, None, :].astype(jnp.float32)).astype(
        jnp.bfloat16
    )
    weighted = weighted.reshape(-1, columns)
    weighted = jnp.concatenate([weighted, jnp.zeros((1, columns), jnp.bfloat16)], axis=0)
    return jnp.take(weighted, source, axis=0).reshape(experts, capacity, columns)


def on_any_tiling(out_grad, gate_probs, expert_ids, gate_pre, up_pre, w_gate, w_up, w_down):
    tokens_here = expert_ids.shape[0]
    experts = lax.axis_size("expert") * w_gate.shape[0]
    groups = gate_pre.shape[1]
    capacity = gate_pre.shape[2]
    units = gate_pre.shape[3]
    local_cols = out_grad.shape[1]
    slot_rows = groups * capacity
    target, source = slot_tables(expert_ids, experts, capacity)
    down_weight = w_down[0]
    contract_last = (((1,), (1,)), ((), ()))
    contract_first = (((0,), (0,)), ((), ()))
    gate_act = gate_pre[0].reshape(slot_rows, units).astype(jnp.float32)
    up_act = up_pre[0].reshape(slot_rows, units).astype(jnp.float32)
    logistic = jax.nn.sigmoid(gate_act)
    hidden_act = (gate_act * logistic * up_act).astype(jnp.bfloat16)
    features = lax.all_gather(out_grad, "cuts", axis=1, tiled=True)
    outgoing = pack_rows(features, gate_probs, source, experts, capacity)
    routed = lax.all_to_all(outgoing, "expert", split_axis=0, concat_axis=0, tiled=True)
    routed = routed.reshape(slot_rows, routed.shape[2])
    hidden_grad = lax.dot_general(
        routed, down_weight, contract_last, preferred_element_type=jnp.float32
    )
    down_grad = lax.dot_general(
        hidden_act, routed, contract_first, preferred_element_type=jnp.float32
    )
    w_down_grad = down_grad.astype(jnp.bfloat16)[None]
    up_grad = (hidden_grad * gate_act * logistic).astype(jnp.bfloat16)
    gate_grad = (hidden_grad * up_act * logistic * (1.0 + gate_act * (1.0 - logistic))).astype(
        jnp.bfloat16
    )
    gate_weight = w_gate[0]
    up_weight = w_up[0]
    partial_value = lax.dot_general(
        gate_weight, gate_grad, contract_last, preferred_element_type=jnp.float32
    )
    partial_value = partial_value + lax.dot_general(
        up_weight, up_grad, contract_last, preferred_element_type=jnp.float32
    )
    summed = lax.psum_scatter(
        lax.optimization_barrier(partial_value.astype(jnp.bfloat16))
        .astype(jnp.float32)
        .astype(jnp.bfloat16),
        "cuts",
        scatter_dimension=0,
        tiled=True,
    ).astype(jnp.float32)
    summed = summed.reshape(local_cols, groups, capacity)
    returned = lax.all_to_all(
        summed.astype(jnp.bfloat16), "expert", split_axis=1, concat_axis=1, tiled=True
    ).astype(summed.dtype)
    flat_back = returned.reshape(local_cols, experts * capacity)
    picked = jnp.take(flat_back, target, axis=1).reshape(local_cols, tokens_here, -1)
    input_grad = jnp.sum(picked, axis=2)
    return (input_grad.T.astype(jnp.bfloat16), w_down_grad)


def on_device(out_grad, gate_probs, expert_ids, gate_pre, up_pre, w_gate, w_up, w_down):
    experts = lax.axis_size("expert")
    cuts = lax.axis_size("cuts")
    line = cuts // 2
    capacity = gate_pre.shape[2]
    if out_grad.shape[1] % 256 or gate_pre.shape[3] % 256 or capacity % 16 or cuts != 8:
        return on_any_tiling(
            out_grad, gate_probs, expert_ids, gate_pre, up_pre, w_gate, w_up, w_down
        )

    def along(x, shift):
        pairs = [(i, (i + 2 * shift) % cuts) for i in range(cuts)]
        return lax.ppermute(x, "cuts", pairs)

    def swap(x):
        return lax.ppermute(x, "cuts", [(i, i ^ 1) for i in range(cuts)])

    def exchange(pieces):
        moved = [
            lax.ppermute(pieces[r], "expert", [(i, i ^ r) for i in range(experts)])
            for r in range(1, experts)
        ]
        return [pieces[0]] + moved

    near = [1, line - 1]
    far = [2]
    raws = [along(out_grad, shift) for shift in near]
    sel, gate, again, *pieces, t = first_pack(
        out_grad, expert_ids.T, gate_probs.T, experts, capacity
    )
    pieces0 = exchange(pieces)
    raw2 = along(again, 2)
    up_factor, gate_factor, act, t = activations(gate_pre, up_pre, [t])
    mine0 = jnp.concatenate(pieces0, axis=1)
    theirs0 = swap(mine0)
    total, t = hidden_part(mine0, w_down, [0], line, False, None, (), [t])
    *pieces, t = pack(raws, sel, gate, experts, capacity, [t])
    pieces1 = exchange(pieces)
    total, t = hidden_part(theirs0, w_down, [0], line, True, total, (), [t])
    down, t = down_part(act, mine0, theirs0, [0], line, None, w_down.shape, [t])
    *pieces, t = pack([raw2], sel, gate, experts, capacity, [t])
    pieces2 = exchange(pieces)
    mine1 = jnp.concatenate(pieces1, axis=1)
    theirs1 = swap(mine1)
    total, t = hidden_part(mine1, w_down, near, line, False, total, (), [t])
    total, t = hidden_part(theirs1, w_down, near, line, True, total, (), [t])
    mine2 = jnp.concatenate(pieces2, axis=1)
    theirs2 = swap(mine2)
    total, t = hidden_part(mine2, w_down, far, line, False, total, (), [t])
    gate_grad, up_grad, t = hidden_part(
        theirs2, w_down, far, line, True, total, (gate_factor, up_factor), [t]
    )

    back = functools.partial(slot_part, gate_grad, up_grad, w_gate, w_up)
    part2, t = back(far, line, True, None, experts, [t])
    other2 = swap(part2)
    part1, t = back(near, line, True, None, experts, [t])
    other1 = swap(part1)
    *send2, t = back(far, line, False, other2, experts, [t])
    got2 = exchange(send2)
    part0, t = back([0], line, True, None, experts, [t])
    other0 = swap(part0)
    far_out, t = combine(got2, sel, [], [t])
    landed = [along(far_out, 2)]
    *send1, t = back(near, line, False, other1, experts, [t])
    got1 = exchange(send1)
    *send0, t = back([0], line, False, other0, experts, [t])
    got0 = exchange(send0)
    down, t = down_part(act, mine1, theirs1, near, line, down, w_down.shape, [t])
    *near_out, t = combine(got1, sel, [], [t])
    landed += [along(part, shift) for part, shift in zip(near_out, near)]
    down, t = down_part(act, mine2, theirs2, far, line, down, w_down.shape, [t])
    result, t = combine(got0, sel, landed, [t])
    return result, down


def solution(mesh):
    return jax.shard_map(
        on_device,
        mesh=mesh,
        in_specs=(
            P("expert", "cuts"),
            P("expert", None),
            P("expert", None),
            P("expert", None, None, "cuts"),
            P("expert", None, None, "cuts"),
            P("expert", None, "cuts"),
            P("expert", None, "cuts"),
            P("expert", "cuts", None),
        ),
        out_specs=(P("expert", "cuts"), P("expert", "cuts", None)),
        check_vma=False,
    )
```

```python
import functools
import jax
import jax.numpy as jnp
from jax import lax
from jax.experimental import pallas as pl
from jax.experimental.pallas import tpu as pltpu
from jax.sharding import PartitionSpec as P

BF16 = jnp.bfloat16
F32 = jnp.float32
VMEM = pl.BlockSpec(memory_space=pltpu.VMEM)
ANY = pl.BlockSpec(memory_space=pl.ANY)
NT = (((1,), (1,)), ((), ()))
TN = (((0,), (0,)), ((), ()))
NN = (((1,), (0,)), ((), ()))
MIB = 1 << 20
ACT_FLOPS = 1.2e10
SMALL = 1e3
DOWN_WEIGHT = 0.0


def dot(a, b, dims):
    return lax.dot_general(a, b, dims, preferred_element_type=F32)


def shaped(shape, dtype):
    return jax.ShapeDtypeStruct(shape, dtype)


def in_hbm(x):
    return pltpu.with_memory_space_constraint(x, pltpu.HBM)


def call(kernel, name, operands, out_shape, after=(), flops=0, moved=0, mib=4, out_specs=None, **more):
    count, extra, results = len(operands), len(after), len(out_shape)

    def body(*refs):
        outs = refs[count + extra :]
        kernel(*refs[:count], *outs[:results], *outs[results + 1 :])
        outs[results][...] = jnp.zeros((8, 128), F32)

    out_shape = list(out_shape) + [shaped((8, 128), F32)]
    out_specs = list(out_specs or [VMEM] * results) + [VMEM]
    specs = more.pop("in_specs", [VMEM] * count)
    return pl.pallas_call(
        body,
        out_shape=out_shape,
        in_specs=list(specs) + [VMEM] * extra,
        out_specs=out_specs,
        compiler_params=pltpu.CompilerParams(vmem_limit_bytes=mib * MIB),
        cost_estimate=pl.CostEstimate(
            flops=int(flops), bytes_accessed=int(moved), transcendentals=0
        ),
        name=name,
        **more,
    )(*operands, *after)


def route(raw, ids, probs, experts, capacity):
    tokens = ids.shape[1]
    lines = max(8, experts)
    rows = experts * capacity

    def kernel(raw_hbm, ids_hbm, probs_hbm, sel_ref, gate_ref, own_ref, ids_ref, probs_ref, sems):
        copies = [
            pltpu.make_async_copy(ids_hbm, ids_ref, sems.at[0]),
            pltpu.make_async_copy(probs_hbm, probs_ref, sems.at[1]),
            pltpu.make_async_copy(raw_hbm, own_ref, sems.at[2]),
        ]
        for copy in copies:
            copy.start()
        before = lax.broadcasted_iota(jnp.int32, (tokens, tokens), 0)
        here = lax.broadcasted_iota(jnp.int32, (tokens, tokens), 1)
        earlier = (before < here).astype(F32).astype(BF16)
        slot = lax.broadcasted_iota(jnp.int32, (capacity, tokens), 0).astype(F32)
        expert = lax.broadcasted_iota(jnp.int32, (lines, tokens), 0) ^ lax.axis_index("expert")
        for copy in copies:
            copy.wait()
        first = (ids_ref[0:1, :] == expert).astype(F32)
        second = (ids_ref[1:2, :] == expert).astype(F32)
        hit = first + second
        place = dot(hit.astype(BF16), earlier, NN)
        place = jnp.where(hit > 0.0, place, -1.0)
        gate = first * probs_ref[0:1, :] + second * probs_ref[1:2, :]
        for r in range(experts):
            match = place[r : r + 1, :] == slot
            span = pl.ds(r * capacity, capacity)
            sel_ref[span, :] = jnp.where(match, 1.0, 0.0).astype(BF16)
            gate_ref[span, :] = jnp.sum(
                jnp.where(match, gate[r : r + 1, :], 0.0), axis=1, keepdims=True
            )

    return call(
        kernel,
        "route",
        [in_hbm(raw), in_hbm(ids), in_hbm(probs)],
        [shaped((rows, tokens), BF16), shaped((rows, 1), F32), shaped(raw.shape, BF16)],
        flops=SMALL,
        moved=SMALL,
        in_specs=[ANY] * 3,
        scratch_shapes=[
            pltpu.VMEM(ids.shape, jnp.int32),
            pltpu.VMEM(probs.shape, F32),
            pltpu.SemaphoreType.DMA((3,)),
        ],
    )


def pack(raws, sel, gate, experts, capacity, after, again=False):
    blocks = len(raws)
    columns = raws[0].shape[1]

    def kernel(*refs):
        sel_ref, gate_ref = refs[blocks : blocks + 2]
        outs = refs[blocks + 2 :]
        for b in range(blocks):
            rows = (dot(sel_ref[...], refs[b][...], NN) * gate_ref[...]).astype(BF16)
            for r, out in enumerate(outs[:experts]):
                out[b] = rows[r * capacity : (r + 1) * capacity]
        if again:
            outs[experts][...] = refs[0][...]

    return call(
        kernel,
        "pack",
        [*raws, sel, gate],
        [shaped((blocks, capacity, columns), BF16)] * experts
        + [shaped(raws[0].shape, BF16)] * again,
        after,
        flops=2 * blocks * sel.shape[0] * sel.shape[1] * columns,
        moved=6e5 * blocks,
    )


def join(pieces, after):
    experts = len(pieces)
    blocks, capacity, columns = pieces[0].shape

    def kernel(*refs):
        for r in range(experts):
            refs[experts][:, pl.ds(r * capacity, capacity), :] = refs[r][...]

    return call(
        kernel, "join", pieces, [shaped((blocks, experts * capacity, columns), BF16)], after
    )


def activations(gate_pre, up_pre, after):
    _, groups, capacity, units = gate_pre.shape
    rows = groups * capacity
    tile = 256

    def kernel(gate_hbm, up_hbm, up_factor, gate_factor, act, gate_ref, up_ref, sems):
        me = lax.axis_index("expert")
        copies = []
        for r in range(groups):
            span = pl.ds(r * capacity, capacity)
            for i, (source, target) in enumerate(((gate_hbm, gate_ref), (up_hbm, up_ref))):
                copies.append(
                    pltpu.make_async_copy(source.at[0, me ^ r], target.at[span, :], sems.at[i, r])
                )
        for copy in copies:
            copy.start()
        for copy in copies:
            copy.wait()

        def step(i, unused):
            span = pl.ds(pl.multiple_of(i * tile, tile), tile)
            a = gate_ref[:, span].astype(F32).T
            b = up_ref[:, span].astype(F32).T
            sig = 1.0 / (1.0 + jnp.exp(-a))
            swish = a * sig
            up_factor[span, :] = swish
            gate_factor[span, :] = b * sig * (1.0 + a * (1.0 - sig))
            act[span, :] = (swish * b).astype(BF16)
            return unused

        lax.fori_loop(0, units // tile, step, 0)

    return call(
        kernel,
        "activations",
        [in_hbm(gate_pre), in_hbm(up_pre)],
        [shaped((units, rows), F32), shaped((units, rows), F32), shaped((units, rows), BF16)],
        after,
        flops=ACT_FLOPS,
        moved=SMALL,
        in_specs=[ANY, ANY],
        scratch_shapes=[
            pltpu.VMEM((rows, units), BF16),
            pltpu.VMEM((rows, units), BF16),
            pltpu.SemaphoreType.DMA((2, groups)),
        ],
    )


def block_of(shift, line, sibling):
    cut = lax.axis_index("cuts")
    z = lax.rem(lax.div(cut, 2) + (shift + line), line)
    core = lax.rem(cut, 2)
    return z * 2 + (1 - core if sibling else core)


def hidden_part(terms, w_down, line, total, factors, after):
    _, rows, columns = terms[0][0].shape
    units = w_down.shape[1]
    count = len(terms)
    has_total = total is not None

    def kernel(*refs):
        w_ref, refs, x_refs = refs[count], refs[count + 1 :], refs[:count]
        outs = refs[has_total + len(factors) :]
        factor_refs = refs[has_total : has_total + len(factors)]
        value = refs[0][...] if has_total else 0.0
        for x_ref, (_, shifts, sibling) in zip(x_refs, terms):
            for b, shift in enumerate(shifts):
                start = pl.multiple_of(block_of(-shift, line, sibling) * columns, 128)
                value = value + dot(w_ref[0, :, pl.ds(start, columns)], x_ref[b], NT)
        if factors:
            for out, factor in zip(outs, factor_refs):
                out[...] = (value * factor[...]).astype(BF16)
        else:
            outs[0][...] = value

    return call(
        kernel,
        "hidden_part",
        [term[0] for term in terms] + [w_down] + ([total] if has_total else []) + list(factors),
        [shaped((units, rows), BF16)] * 2 if factors else [shaped((units, rows), F32)],
        after,
        moved=SMALL,
        flops=SMALL,
    )


def down_part(act, mine, theirs, shifts, line, before, out_shape, after, weight=1.0):
    blocks, rows, columns = mine.shape
    units = act.shape[0]
    split = 2
    slots = 3
    part = units // split
    steps = [(half, b) for half in range(2) for b in range(blocks)]

    def kernel(act_ref, mine_ref, theirs_ref, *refs):
        out_ref, held, sems = refs[-3:]
        copies = []
        for i, (half, b) in enumerate(steps):
            start = pl.multiple_of(block_of(-shifts[b], line, bool(half)) * columns, 128)
            now = i % slots
            x = (theirs_ref if half else mine_ref)[b]
            for j in range(split):
                if i >= slots:
                    copies[(i - slots) * split + j].wait()
                span = pl.ds(j * part, part)
                held[now, span, :] = dot(act_ref[span, :], x, NN).astype(BF16)
                copy = pltpu.make_async_copy(
                    held.at[now, span, :],
                    out_ref.at[0, span, pl.ds(start, columns)],
                    sems.at[now, j],
                )
                copy.start()
                copies.append(copy)
        for copy in copies[-slots * split :]:
            copy.wait()

    operands = [act, mine, theirs]
    if before is not None:
        operands.append(before)
    return call(
        kernel,
        "down_part",
        operands,
        [shaped(out_shape, BF16)],
        after,
        flops=weight * 4 * blocks * rows * columns * units,
        moved=weight * 4 * blocks * columns * units,
        mib=6,
        in_specs=[VMEM] * 3 + [ANY] * (len(operands) - 3),
        out_specs=[ANY],
        input_output_aliases={} if before is None else {3: 0},
        scratch_shapes=[
            pltpu.VMEM((slots, units, columns), BF16),
            pltpu.SemaphoreType.DMA((slots, split)),
        ],
    )


def slot_part(gate_grad, up_grad, w_gate, w_up, shifts, line, sibling, arrived, experts, after):
    units, rows = gate_grad.shape
    blocks = len(shifts)
    columns = w_gate.shape[1] // (2 * line)
    tile = 256
    capacity = rows // experts
    split = arrived is not None

    def kernel(gate_ref, up_ref, wg_ref, wu_ref, *refs):
        for b, shift in enumerate(shifts):
            base = block_of(shift, line, sibling) * columns
            for i in range(columns // tile):
                span = pl.ds(pl.multiple_of(base + i * tile, tile), tile)
                value = dot(wg_ref[0, span, :], gate_ref[...], NN)
                value = (value + dot(wu_ref[0, span, :], up_ref[...], NN)).T
                out = pl.ds(i * tile, tile)
                if not split:
                    refs[0][b, :, out] = value.astype(BF16)
                    continue
                value = (value + refs[0][b, :, out].astype(F32)).astype(BF16)
                for r in range(experts):
                    refs[1 + r][b, :, out] = value[r * capacity : (r + 1) * capacity]

    if split:
        out_shape = [shaped((blocks, capacity, columns), BF16)] * experts
    else:
        out_shape = [shaped((blocks, rows, columns), BF16)]
    return call(
        kernel,
        "slot_part",
        [gate_grad, up_grad, w_gate, w_up] + ([arrived] if split else []),
        out_shape,
        after,
        flops=4 * blocks * rows * columns * units,
        moved=4 * blocks * columns * units + 4 * rows * units,
    )


def combine(pieces, sel, others, dtypes, after):
    experts = len(pieces)
    blocks, _, columns = pieces[0].shape
    tokens = sel.shape[1]
    flat = [x for group in others for x in group]

    def kernel(*refs):
        piece_refs, sel_ref = refs[:experts], refs[experts]
        other_refs = list(refs[experts + 1 : experts + 1 + len(flat)])
        out_refs = refs[experts + 1 + len(flat) :]
        for b in range(blocks):
            rows = jnp.concatenate([piece[b] for piece in piece_refs], axis=0)
            value = dot(sel_ref[...], rows, TN)
            for _ in others[b]:
                value = value + other_refs.pop(0)[...].astype(F32)
            out_refs[b][...] = value.astype(dtypes[b])

    return call(
        kernel,
        "combine",
        [*pieces, sel, *flat],
        [shaped((tokens, columns), dtype) for dtype in dtypes],
        after,
        flops=2 * blocks * sel.shape[0] * tokens * columns,
        moved=6e5 * blocks,
    )


def slot_tables(routing, experts, capacity):
    chosen = routing.reshape(-1)
    onehot = (chosen[:, None] == jnp.arange(experts, dtype=jnp.int32)[None, :]).astype(jnp.int32)
    earlier = jnp.cumsum(onehot, axis=0) - onehot
    position = jnp.sum(earlier * onehot, axis=1)
    target = chosen * capacity + position
    source = jnp.full((experts * capacity,), chosen.shape[0], jnp.int32)
    source = source.at[target].set(jnp.arange(chosen.shape[0], dtype=jnp.int32))
    return (target, source)


def pack_rows(out_rows, gate_values, source, experts, capacity):
    columns = out_rows.shape[1]
    weighted = (gate_values[:, :, None] * out_rows[:, None, :].astype(jnp.float32)).astype(
        jnp.bfloat16
    )
    weighted = weighted.reshape(-1, columns)
    weighted = jnp.concatenate([weighted, jnp.zeros((1, columns), jnp.bfloat16)], axis=0)
    return jnp.take(weighted, source, axis=0).reshape(experts, capacity, columns)


def on_any_tiling(out_grad, gate_probs, expert_ids, gate_pre, up_pre, w_gate, w_up, w_down):
    tokens_here = expert_ids.shape[0]
    experts = lax.axis_size("expert") * w_gate.shape[0]
    groups = gate_pre.shape[1]
    capacity = gate_pre.shape[2]
    units = gate_pre.shape[3]
    local_cols = out_grad.shape[1]
    slot_rows = groups * capacity
    target, source = slot_tables(expert_ids, experts, capacity)
    down_weight = w_down[0]
    contract_last = (((1,), (1,)), ((), ()))
    contract_first = (((0,), (0,)), ((), ()))
    gate_act = gate_pre[0].reshape(slot_rows, units).astype(jnp.float32)
    up_act = up_pre[0].reshape(slot_rows, units).astype(jnp.float32)
    logistic = jax.nn.sigmoid(gate_act)
    hidden_act = (gate_act * logistic * up_act).astype(jnp.bfloat16)
    features = lax.all_gather(out_grad, "cuts", axis=1, tiled=True)
    outgoing = pack_rows(features, gate_probs, source, experts, capacity)
    routed = lax.all_to_all(outgoing, "expert", split_axis=0, concat_axis=0, tiled=True)
    routed = routed.reshape(slot_rows, routed.shape[2])
    hidden_grad = lax.dot_general(
        routed, down_weight, contract_last, preferred_element_type=jnp.float32
    )
    down_grad = lax.dot_general(
        hidden_act, routed, contract_first, preferred_element_type=jnp.float32
    )
    w_down_grad = down_grad.astype(jnp.bfloat16)[None]
    up_grad = (hidden_grad * gate_act * logistic).astype(jnp.bfloat16)
    gate_grad = (hidden_grad * up_act * logistic * (1.0 + gate_act * (1.0 - logistic))).astype(
        jnp.bfloat16
    )
    gate_weight = w_gate[0]
    up_weight = w_up[0]
    partial_value = lax.dot_general(
        gate_weight, gate_grad, contract_last, preferred_element_type=jnp.float32
    )
    partial_value = partial_value + lax.dot_general(
        up_weight, up_grad, contract_last, preferred_element_type=jnp.float32
    )
    summed = lax.psum_scatter(
        lax.optimization_barrier(partial_value.astype(jnp.bfloat16))
        .astype(jnp.float32)
        .astype(jnp.bfloat16),
        "cuts",
        scatter_dimension=0,
        tiled=True,
    ).astype(jnp.float32)
    summed = summed.reshape(local_cols, groups, capacity)
    returned = lax.all_to_all(
        summed.astype(jnp.bfloat16), "expert", split_axis=1, concat_axis=1, tiled=True
    ).astype(summed.dtype)
    flat_back = returned.reshape(local_cols, experts * capacity)
    picked = jnp.take(flat_back, target, axis=1).reshape(local_cols, tokens_here, -1)
    input_grad = jnp.sum(picked, axis=2)
    return (input_grad.T.astype(jnp.bfloat16), w_down_grad)


def on_device(out_grad, gate_probs, expert_ids, gate_pre, up_pre, w_gate, w_up, w_down):
    experts = lax.axis_size("expert")
    cuts = lax.axis_size("cuts")
    line = cuts // 2
    capacity = gate_pre.shape[2]
    if out_grad.shape[1] % 256 or gate_pre.shape[3] % 256 or capacity % 16 or cuts != 8:
        return on_any_tiling(
            out_grad, gate_probs, expert_ids, gate_pre, up_pre, w_gate, w_up, w_down
        )

    def along(x, shift):
        pairs = [(i, (i + 2 * shift) % cuts) for i in range(cuts)]
        return lax.ppermute(x, "cuts", pairs)

    def swap(x):
        return lax.ppermute(x, "cuts", [(i, i ^ 1) for i in range(cuts)])

    def exchange(pieces):
        moved = {
            r: lax.ppermute(pieces[r], "expert", [(i, i ^ r) for i in range(experts)])
            for r in range(experts - 1, 0, -1)
        }
        return [pieces[0]] + [moved[r] for r in range(1, experts)]

    raw1 = along(out_grad, 1)
    raw2 = along(raw1, 1)
    raw3 = along(out_grad, 3)
    one, two = [0, 1], [3, 2]
    sel, gate, own, t = route(out_grad, expert_ids.T, gate_probs.T, experts, capacity)
    *pieces, t = pack([own, raw1], sel, gate, experts, capacity, [t])
    pieces = exchange(pieces)
    *pieces2, t = pack([raw3, raw2], sel, gate, experts, capacity, [t])
    pieces2 = exchange(pieces2)
    up_factor, gate_factor, act, t = activations(gate_pre, up_pre, [t])
    mine1, t = join(pieces, [t])
    theirs1 = swap(mine1)
    mine2, t = join(pieces2, [t])
    theirs2 = swap(mine2)
    total, t = hidden_part(
        [(mine1, one, False), (theirs1, one, True), (mine2, two, False)],
        w_down, line, None, (), [t],
    )
    gate_grad, up_grad, t = hidden_part(
        [(theirs2, two, True)], w_down, line, total, (gate_factor, up_factor), [t, w_gate]
    )

    first, last = [2, 3], [1, 0]
    back = functools.partial(slot_part, gate_grad, up_grad, w_gate, w_up)
    part, t = back(first, line, True, None, experts, [t])
    other1 = swap(part)
    part, t = back(last, line, True, None, experts, [t])
    other2 = swap(part)
    *pieces, t = back(first, line, False, other1, experts, [t])
    got1 = exchange(pieces)
    *pieces, t = back(last, line, False, other2, experts, [t])
    got2 = exchange(pieces)
    part2, part3, t = combine(got1, sel, [[], []], [BF16, BF16], [t])
    landed2 = along(part2, 1)
    landed3 = along(part3, 3)
    down, t = down_part(act, mine1, theirs1, one, line, None, w_down.shape, [t])
    part1, part0, t = combine(got2, sel, [[landed2], [landed3]], [BF16, F32], [t])
    landed1 = along(part1, 1)
    down, t = down_part(act, mine2, theirs2, two, line, down, w_down.shape, [t], DOWN_WEIGHT)
    result = (part0 + landed1.astype(F32)).astype(BF16)
    return result, down


def solution(mesh):
    return jax.shard_map(
        on_device,
        mesh=mesh,
        in_specs=(
            P("expert", "cuts"),
            P("expert", None),
            P("expert", None),
            P("expert", None, None, "cuts"),
            P("expert", None, None, "cuts"),
            P("expert", None, "cuts"),
            P("expert", None, "cuts"),
            P("expert", "cuts", None),
        ),
        out_specs=(P("expert", "cuts"), P("expert", "cuts", None)),
        check_vma=False,
    )
```

```python
import functools
import jax
import jax.numpy as jnp
from jax import lax
from jax.experimental import pallas as pl
from jax.experimental.pallas import tpu as pltpu
from jax.sharding import PartitionSpec as P

BF16 = jnp.bfloat16
F32 = jnp.float32
VMEM = pl.BlockSpec(memory_space=pltpu.VMEM)
ANY = pl.BlockSpec(memory_space=pl.ANY)
NT = (((1,), (1,)), ((), ()))
TN = (((0,), (0,)), ((), ()))
NN = (((1,), (0,)), ((), ()))
MIB = 1 << 20
ACT_FLOPS = 1.2e10
SMALL = 1e3
DOWN_WEIGHT = 0.0


def dot(a, b, dims):
    return lax.dot_general(a, b, dims, preferred_element_type=F32)


def shaped(shape, dtype):
    return jax.ShapeDtypeStruct(shape, dtype)


def in_hbm(x):
    return pltpu.with_memory_space_constraint(x, pltpu.HBM)


def call(kernel, name, operands, out_shape, after=(), flops=0, moved=0, mib=4, out_specs=None, **more):
    count, extra, results = len(operands), len(after), len(out_shape)

    def body(*refs):
        outs = refs[count + extra :]
        kernel(*refs[:count], *outs[:results], *outs[results + 1 :])
        outs[results][...] = jnp.zeros((8, 128), F32)

    out_shape = list(out_shape) + [shaped((8, 128), F32)]
    out_specs = list(out_specs or [VMEM] * results) + [VMEM]
    specs = more.pop("in_specs", [VMEM] * count)
    return pl.pallas_call(
        body,
        out_shape=out_shape,
        in_specs=list(specs) + [VMEM] * extra,
        out_specs=out_specs,
        compiler_params=pltpu.CompilerParams(vmem_limit_bytes=mib * MIB),
        cost_estimate=pl.CostEstimate(
            flops=int(flops), bytes_accessed=int(moved), transcendentals=0
        ),
        name=name,
        **more,
    )(*operands, *after)


def route(raw, ids, probs, experts, capacity):
    tokens = ids.shape[1]
    lines = max(8, experts)
    rows = experts * capacity

    def kernel(raw_hbm, ids_hbm, probs_hbm, sel_ref, gate_ref, own_ref, ids_ref, probs_ref, sems):
        copies = [
            pltpu.make_async_copy(ids_hbm, ids_ref, sems.at[0]),
            pltpu.make_async_copy(probs_hbm, probs_ref, sems.at[1]),
            pltpu.make_async_copy(raw_hbm, own_ref, sems.at[2]),
        ]
        for copy in copies:
            copy.start()
        before = lax.broadcasted_iota(jnp.int32, (tokens, tokens), 0)
        here = lax.broadcasted_iota(jnp.int32, (tokens, tokens), 1)
        earlier = (before < here).astype(F32).astype(BF16)
        slot = lax.broadcasted_iota(jnp.int32, (capacity, tokens), 0).astype(F32)
        expert = lax.broadcasted_iota(jnp.int32, (lines, tokens), 0) ^ lax.axis_index("expert")
        for copy in copies:
            copy.wait()
        first = (ids_ref[0:1, :] == expert).astype(F32)
        second = (ids_ref[1:2, :] == expert).astype(F32)
        hit = first + second
        place = dot(hit.astype(BF16), earlier, NN)
        place = jnp.where(hit > 0.0, place, -1.0)
        gate = first * probs_ref[0:1, :] + second * probs_ref[1:2, :]
        for r in range(experts):
            match = place[r : r + 1, :] == slot
            span = pl.ds(r * capacity, capacity)
            sel_ref[span, :] = jnp.where(match, 1.0, 0.0).astype(BF16)
            gate_ref[span, :] = jnp.sum(
                jnp.where(match, gate[r : r + 1, :], 0.0), axis=1, keepdims=True
            )

    return call(
        kernel,
        "route",
        [in_hbm(raw), in_hbm(ids), in_hbm(probs)],
        [shaped((rows, tokens), BF16), shaped((rows, 1), F32), shaped(raw.shape, BF16)],
        flops=SMALL,
        moved=SMALL,
        in_specs=[ANY] * 3,
        scratch_shapes=[
            pltpu.VMEM(ids.shape, jnp.int32),
            pltpu.VMEM(probs.shape, F32),
            pltpu.SemaphoreType.DMA((3,)),
        ],
    )


def pack(raws, sel, gate, experts, capacity, after, again=False):
    blocks = len(raws)
    columns = raws[0].shape[1]

    def kernel(*refs):
        sel_ref, gate_ref = refs[blocks : blocks + 2]
        outs = refs[blocks + 2 :]
        for b in range(blocks):
            rows = (dot(sel_ref[...], refs[b][...], NN) * gate_ref[...]).astype(BF16)
            for r, out in enumerate(outs[:experts]):
                out[b] = rows[r * capacity : (r + 1) * capacity]
        if again:
            outs[experts][...] = refs[0][...]

    return call(
        kernel,
        "pack",
        [*raws, sel, gate],
        [shaped((blocks, capacity, columns), BF16)] * experts
        + [shaped(raws[0].shape, BF16)] * again,
        after,
        flops=2 * blocks * sel.shape[0] * sel.shape[1] * columns,
        moved=6e5 * blocks,
    )


def join(pieces, after):
    experts = len(pieces)
    blocks, capacity, columns = pieces[0].shape

    def kernel(*refs):
        for r in range(experts):
            refs[experts][:, pl.ds(r * capacity, capacity), :] = refs[r][...]

    return call(
        kernel, "join", pieces, [shaped((blocks, experts * capacity, columns), BF16)], after
    )


def activations(gate_pre, up_pre, after):
    _, groups, capacity, units = gate_pre.shape
    rows = groups * capacity
    tile = 256

    def kernel(gate_hbm, up_hbm, up_factor, gate_factor, act, gate_ref, up_ref, sems):
        me = lax.axis_index("expert")
        copies = []
        for r in range(groups):
            span = pl.ds(r * capacity, capacity)
            for i, (source, target) in enumerate(((gate_hbm, gate_ref), (up_hbm, up_ref))):
                copies.append(
                    pltpu.make_async_copy(source.at[0, me ^ r], target.at[span, :], sems.at[i, r])
                )
        for copy in copies:
            copy.start()
        for copy in copies:
            copy.wait()

        def step(i, unused):
            span = pl.ds(pl.multiple_of(i * tile, tile), tile)
            a = gate_ref[:, span].astype(F32).T
            b = up_ref[:, span].astype(F32).T
            sig = 1.0 / (1.0 + jnp.exp(-a))
            swish = a * sig
            up_factor[span, :] = swish
            gate_factor[span, :] = b * sig * (1.0 + a * (1.0 - sig))
            act[span, :] = (swish * b).astype(BF16)
            return unused

        lax.fori_loop(0, units // tile, step, 0)

    return call(
        kernel,
        "activations",
        [in_hbm(gate_pre), in_hbm(up_pre)],
        [shaped((units, rows), F32), shaped((units, rows), F32), shaped((units, rows), BF16)],
        after,
        flops=ACT_FLOPS,
        moved=SMALL,
        in_specs=[ANY, ANY],
        scratch_shapes=[
            pltpu.VMEM((rows, units), BF16),
            pltpu.VMEM((rows, units), BF16),
            pltpu.SemaphoreType.DMA((2, groups)),
        ],
    )


def ring(line):
    return [*range(0, line, 2), *range(line - 1 - line % 2, 0, -2)]


def block_of(shift, line, sibling):
    cut = lax.axis_index("cuts")
    core = lax.rem(cut, 2)
    z = lax.div(cut, 2)
    order = ring(line)
    ahead = jnp.int32(0)
    for i, place in enumerate(order):
        ahead = jnp.where(z == place, order[(i + shift) % line], ahead)
    return ahead * 2 + (1 - core if sibling else core)


def hidden_part(terms, w_down, line, total, factors, after):
    _, rows, columns = terms[0][0].shape
    units = w_down.shape[1]
    count = len(terms)
    has_total = total is not None

    def kernel(*refs):
        w_ref, refs, x_refs = refs[count], refs[count + 1 :], refs[:count]
        outs = refs[has_total + len(factors) :]
        factor_refs = refs[has_total : has_total + len(factors)]
        value = refs[0][...] if has_total else 0.0
        for x_ref, (_, shifts, sibling) in zip(x_refs, terms):
            for b, shift in enumerate(shifts):
                start = pl.multiple_of(block_of(-shift, line, sibling) * columns, 128)
                value = value + dot(w_ref[0, :, pl.ds(start, columns)], x_ref[b], NT)
        if factors:
            for out, factor in zip(outs, factor_refs):
                out[...] = (value * factor[...]).astype(BF16)
        else:
            outs[0][...] = value

    return call(
        kernel,
        "hidden_part",
        [term[0] for term in terms] + [w_down] + ([total] if has_total else []) + list(factors),
        [shaped((units, rows), BF16)] * 2 if factors else [shaped((units, rows), F32)],
        after,
        moved=SMALL,
        flops=SMALL,
    )


def down_part(act, mine, theirs, shifts, line, before, out_shape, after, weight=1.0):
    blocks, rows, columns = mine.shape
    units = act.shape[0]
    split = 2
    slots = 3
    part = units // split
    steps = [(half, b) for half in range(2) for b in range(blocks)]

    def kernel(act_ref, mine_ref, theirs_ref, *refs):
        out_ref, held, sems = refs[-3:]
        copies = []
        for i, (half, b) in enumerate(steps):
            start = pl.multiple_of(block_of(-shifts[b], line, bool(half)) * columns, 128)
            now = i % slots
            x = (theirs_ref if half else mine_ref)[b]
            for j in range(split):
                if i >= slots:
                    copies[(i - slots) * split + j].wait()
                span = pl.ds(j * part, part)
                held[now, span, :] = dot(act_ref[span, :], x, NN).astype(BF16)
                copy = pltpu.make_async_copy(
                    held.at[now, span, :],
                    out_ref.at[0, span, pl.ds(start, columns)],
                    sems.at[now, j],
                )
                copy.start()
                copies.append(copy)
        for copy in copies[-slots * split :]:
            copy.wait()

    operands = [act, mine, theirs]
    if before is not None:
        operands.append(before)
    return call(
        kernel,
        "down_part",
        operands,
        [shaped(out_shape, BF16)],
        after,
        flops=weight * 4 * blocks * rows * columns * units,
        moved=weight * 4 * blocks * columns * units,
        mib=6,
        in_specs=[VMEM] * 3 + [ANY] * (len(operands) - 3),
        out_specs=[ANY],
        input_output_aliases={} if before is None else {3: 0},
        scratch_shapes=[
            pltpu.VMEM((slots, units, columns), BF16),
            pltpu.SemaphoreType.DMA((slots, split)),
        ],
    )


def slot_part(gate_grad, up_grad, w_gate, w_up, shifts, line, sibling, after):
    units, rows = gate_grad.shape
    blocks = len(shifts)
    columns = w_gate.shape[1] // (2 * line)
    tile = 256
    dtype = BF16 if sibling else F32

    def kernel(gate_ref, up_ref, wg_ref, wu_ref, out_ref):
        for b, shift in enumerate(shifts):
            base = block_of(shift, line, sibling) * columns
            for i in range(columns // tile):
                span = pl.ds(pl.multiple_of(base + i * tile, tile), tile)
                value = dot(wg_ref[0, span, :], gate_ref[...], NN)
                value = value + dot(wu_ref[0, span, :], up_ref[...], NN)
                out_ref[b, :, pl.ds(i * tile, tile)] = value.T.astype(dtype)

    return call(
        kernel,
        "slot_part",
        [gate_grad, up_grad, w_gate, w_up],
        [shaped((blocks, rows, columns), dtype)],
        after,
        flops=4 * blocks * rows * columns * units,
        moved=4 * blocks * columns * units + 4 * rows * units,
    )


def add_halves(own, arrived, experts, after):
    blocks, rows, columns = own.shape
    capacity = rows // experts

    def kernel(own_ref, other_ref, *outs):
        for b in range(blocks):
            for r in range(experts):
                span = pl.ds(r * capacity, capacity)
                value = own_ref[b, span, :] + other_ref[b, span, :].astype(F32)
                outs[r][b] = value.astype(BF16)

    return call(
        kernel,
        "add_halves",
        [own, arrived],
        [shaped((blocks, capacity, columns), BF16)] * experts,
        after,
        moved=SMALL,
        flops=SMALL,
    )


def combine(pieces, sel, others, dtypes, after):
    experts = len(pieces)
    blocks, _, columns = pieces[0].shape
    tokens = sel.shape[1]
    flat = [x for group in others for x in group]

    def kernel(*refs):
        piece_refs, sel_ref = refs[:experts], refs[experts]
        other_refs = list(refs[experts + 1 : experts + 1 + len(flat)])
        out_refs = refs[experts + 1 + len(flat) :]
        for b in range(blocks):
            rows = jnp.concatenate([piece[b] for piece in piece_refs], axis=0)
            value = dot(sel_ref[...], rows, TN)
            for _ in others[b]:
                value = value + other_refs.pop(0)[...].astype(F32)
            out_refs[b][...] = value.astype(dtypes[b])

    return call(
        kernel,
        "combine",
        [*pieces, sel, *flat],
        [shaped((tokens, columns), dtype) for dtype in dtypes],
        after,
        flops=2 * blocks * sel.shape[0] * tokens * columns,
        moved=6e5 * blocks,
    )


def slot_tables(routing, experts, capacity):
    chosen = routing.reshape(-1)
    onehot = (chosen[:, None] == jnp.arange(experts, dtype=jnp.int32)[None, :]).astype(jnp.int32)
    earlier = jnp.cumsum(onehot, axis=0) - onehot
    position = jnp.sum(earlier * onehot, axis=1)
    target = chosen * capacity + position
    source = jnp.full((experts * capacity,), chosen.shape[0], jnp.int32)
    source = source.at[target].set(jnp.arange(chosen.shape[0], dtype=jnp.int32))
    return (target, source)


def pack_rows(out_rows, gate_values, source, experts, capacity):
    columns = out_rows.shape[1]
    weighted = (gate_values[:, :, None] * out_rows[:, None, :].astype(jnp.float32)).astype(
        jnp.bfloat16
    )
    weighted = weighted.reshape(-1, columns)
    weighted = jnp.concatenate([weighted, jnp.zeros((1, columns), jnp.bfloat16)], axis=0)
    return jnp.take(weighted, source, axis=0).reshape(experts, capacity, columns)


def on_any_tiling(out_grad, gate_probs, expert_ids, gate_pre, up_pre, w_gate, w_up, w_down):
    tokens_here = expert_ids.shape[0]
    experts = lax.axis_size("expert") * w_gate.shape[0]
    groups = gate_pre.shape[1]
    capacity = gate_pre.shape[2]
    units = gate_pre.shape[3]
    local_cols = out_grad.shape[1]
    slot_rows = groups * capacity
    target, source = slot_tables(expert_ids, experts, capacity)
    down_weight = w_down[0]
    contract_last = (((1,), (1,)), ((), ()))
    contract_first = (((0,), (0,)), ((), ()))
    gate_act = gate_pre[0].reshape(slot_rows, units).astype(jnp.float32)
    up_act = up_pre[0].reshape(slot_rows, units).astype(jnp.float32)
    logistic = jax.nn.sigmoid(gate_act)
    hidden_act = (gate_act * logistic * up_act).astype(jnp.bfloat16)
    features = lax.all_gather(out_grad, "cuts", axis=1, tiled=True)
    outgoing = pack_rows(features, gate_probs, source, experts, capacity)
    routed = lax.all_to_all(outgoing, "expert", split_axis=0, concat_axis=0, tiled=True)
    routed = routed.reshape(slot_rows, routed.shape[2])
    hidden_grad = lax.dot_general(
        routed, down_weight, contract_last, preferred_element_type=jnp.float32
    )
    down_grad = lax.dot_general(
        hidden_act, routed, contract_first, preferred_element_type=jnp.float32
    )
    w_down_grad = down_grad.astype(jnp.bfloat16)[None]
    up_grad = (hidden_grad * gate_act * logistic).astype(jnp.bfloat16)
    gate_grad = (hidden_grad * up_act * logistic * (1.0 + gate_act * (1.0 - logistic))).astype(
        jnp.bfloat16
    )
    gate_weight = w_gate[0]
    up_weight = w_up[0]
    partial_value = lax.dot_general(
        gate_weight, gate_grad, contract_last, preferred_element_type=jnp.float32
    )
    partial_value = partial_value + lax.dot_general(
        up_weight, up_grad, contract_last, preferred_element_type=jnp.float32
    )
    summed = lax.psum_scatter(
        lax.optimization_barrier(partial_value.astype(jnp.bfloat16))
        .astype(jnp.float32)
        .astype(jnp.bfloat16),
        "cuts",
        scatter_dimension=0,
        tiled=True,
    ).astype(jnp.float32)
    summed = summed.reshape(local_cols, groups, capacity)
    returned = lax.all_to_all(
        summed.astype(jnp.bfloat16), "expert", split_axis=1, concat_axis=1, tiled=True
    ).astype(summed.dtype)
    flat_back = returned.reshape(local_cols, experts * capacity)
    picked = jnp.take(flat_back, target, axis=1).reshape(local_cols, tokens_here, -1)
    input_grad = jnp.sum(picked, axis=2)
    return (input_grad.T.astype(jnp.bfloat16), w_down_grad)


def on_device(out_grad, gate_probs, expert_ids, gate_pre, up_pre, w_gate, w_up, w_down):
    experts = lax.axis_size("expert")
    cuts = lax.axis_size("cuts")
    line = cuts // 2
    capacity = gate_pre.shape[2]
    if out_grad.shape[1] % 256 or gate_pre.shape[3] % 256 or capacity % 16 or cuts != 8:
        return on_any_tiling(
            out_grad, gate_probs, expert_ids, gate_pre, up_pre, w_gate, w_up, w_down
        )

    def along(x, shift):
        order = ring(line)
        pairs = [
            (2 * order[i] + core, 2 * order[(i + shift) % line] + core)
            for i in range(line)
            for core in range(2)
        ]
        return lax.ppermute(x, "cuts", pairs)

    def swap(x):
        return lax.ppermute(x, "cuts", [(i, i ^ 1) for i in range(cuts)])

    def exchange(pieces):
        moved = {
            r: lax.ppermute(pieces[r], "expert", [(i, i ^ r) for i in range(experts)])
            for r in range(experts - 1, 0, -1)
        }
        return [pieces[0]] + [moved[r] for r in range(1, experts)]

    raw1 = along(out_grad, 1)
    raw2 = along(raw1, 1)
    raw3 = along(out_grad, 3)
    one, two = [0, 1], [3, 2]
    sel, gate, own, t = route(out_grad, expert_ids.T, gate_probs.T, experts, capacity)
    *pieces, t = pack([own, raw1], sel, gate, experts, capacity, [t])
    pieces = exchange(pieces)
    *pieces2, t = pack([raw3, raw2], sel, gate, experts, capacity, [t])
    pieces2 = exchange(pieces2)
    up_factor, gate_factor, act, t = activations(gate_pre, up_pre, [t])
    mine1, t = join(pieces, [t])
    theirs1 = swap(mine1)
    mine2, t = join(pieces2, [t])
    theirs2 = swap(mine2)
    total, t = hidden_part(
        [(mine1, one, False), (theirs1, one, True), (mine2, two, False)],
        w_down, line, None, (), [t],
    )
    gate_grad, up_grad, t = hidden_part(
        [(theirs2, two, True)], w_down, line, total, (gate_factor, up_factor), [t, w_gate]
    )

    first, last = [2, 3], [1, 0]
    back = functools.partial(slot_part, gate_grad, up_grad, w_gate, w_up)
    def exchanged(shifts, t):
        part, t = back(shifts, line, True, [t])
        arrived = swap(part)
        part, t = back(shifts, line, False, [t])
        *pieces, t = add_halves(part, arrived, experts, [t])
        return exchange(pieces), t

    got1, t = exchanged(first, t)
    got2, t = exchanged(last, t)
    part2, part3, t = combine(got1, sel, [[], []], [BF16, BF16], [t])
    landed2 = along(part2, 1)
    landed3 = along(part3, 3)
    down, t = down_part(act, mine1, theirs1, one, line, None, w_down.shape, [t])
    part1, part0, t = combine(got2, sel, [[landed2], []], [BF16, F32], [t])
    landed1 = along(part1, 1)
    down, t = down_part(act, mine2, theirs2, two, line, down, w_down.shape, [t], DOWN_WEIGHT)
    result = (part0 + landed3.astype(F32) + landed1.astype(F32)).astype(BF16)
    return result, down


def solution(mesh):
    return jax.shard_map(
        on_device,
        mesh=mesh,
        in_specs=(
            P("expert", "cuts"),
            P("expert", None),
            P("expert", None),
            P("expert", None, None, "cuts"),
            P("expert", None, None, "cuts"),
            P("expert", None, "cuts"),
            P("expert", None, "cuts"),
            P("expert", "cuts", None),
        ),
        out_specs=(P("expert", "cuts"), P("expert", "cuts", None)),
        check_vma=False,
    )
```

```python
import functools
import jax
import jax.numpy as jnp
from jax import lax
from jax.experimental import pallas as pl
from jax.experimental.pallas import tpu as pltpu
from jax.sharding import PartitionSpec as P

BF16 = jnp.bfloat16
F32 = jnp.float32
VMEM = pl.BlockSpec(memory_space=pltpu.VMEM)
ANY = pl.BlockSpec(memory_space=pl.ANY)
NT = (((1,), (1,)), ((), ()))
TN = (((0,), (0,)), ((), ()))
NN = (((1,), (0,)), ((), ()))
MIB = 1 << 20
ACT_FLOPS = 1.2e10
SMALL = 1e3
DOWN_WEIGHT = 0.0


def dot(a, b, dims):
    return lax.dot_general(a, b, dims, preferred_element_type=F32)


def shaped(shape, dtype):
    return jax.ShapeDtypeStruct(shape, dtype)


def in_hbm(x):
    return pltpu.with_memory_space_constraint(x, pltpu.HBM)


def call(kernel, name, operands, out_shape, after=(), flops=0, moved=0, mib=4, out_specs=None, **more):
    count, extra, results = len(operands), len(after), len(out_shape)

    def body(*refs):
        outs = refs[count + extra :]
        kernel(*refs[:count], *outs[:results], *outs[results + 1 :])
        outs[results][...] = jnp.zeros((8, 128), F32)

    out_shape = list(out_shape) + [shaped((8, 128), F32)]
    out_specs = list(out_specs or [VMEM] * results) + [VMEM]
    specs = more.pop("in_specs", [VMEM] * count)
    return pl.pallas_call(
        body,
        out_shape=out_shape,
        in_specs=list(specs) + [VMEM] * extra,
        out_specs=out_specs,
        compiler_params=pltpu.CompilerParams(vmem_limit_bytes=mib * MIB),
        cost_estimate=pl.CostEstimate(
            flops=int(flops), bytes_accessed=int(moved), transcendentals=0
        ),
        name=name,
        **more,
    )(*operands, *after)


def codes(experts):
    return [0, *sorted(range(1, experts), key=lambda code: (-bin(code).count("1"), code))]


def route(raw, ids, probs, experts, capacity):
    tokens = ids.shape[1]
    lines = max(8, experts)
    rows = experts * capacity

    def kernel(raw_hbm, ids_hbm, probs_hbm, sel_ref, gate_ref, own_ref, ids_ref, probs_ref, sems):
        copies = [
            pltpu.make_async_copy(ids_hbm, ids_ref, sems.at[0]),
            pltpu.make_async_copy(probs_hbm, probs_ref, sems.at[1]),
            pltpu.make_async_copy(raw_hbm, own_ref, sems.at[2]),
        ]
        for copy in copies:
            copy.start()
        before = lax.broadcasted_iota(jnp.int32, (tokens, tokens), 0)
        here = lax.broadcasted_iota(jnp.int32, (tokens, tokens), 1)
        earlier = (before < here).astype(F32).astype(BF16)
        slot = lax.broadcasted_iota(jnp.int32, (capacity, tokens), 0).astype(F32)
        line = lax.broadcasted_iota(jnp.int32, (lines, tokens), 0)
        expert = jnp.full((lines, tokens), experts, jnp.int32)
        for r, code in enumerate(codes(experts)):
            expert = jnp.where(line == r, lax.axis_index("expert") ^ code, expert)
        for copy in copies:
            copy.wait()
        first = (ids_ref[0:1, :] == expert).astype(F32)
        second = (ids_ref[1:2, :] == expert).astype(F32)
        hit = first + second
        place = dot(hit.astype(BF16), earlier, NN)
        place = jnp.where(hit > 0.0, place, -1.0)
        gate = first * probs_ref[0:1, :] + second * probs_ref[1:2, :]
        for r in range(experts):
            match = place[r : r + 1, :] == slot
            span = pl.ds(r * capacity, capacity)
            sel_ref[span, :] = jnp.where(match, 1.0, 0.0).astype(BF16)
            gate_ref[span, :] = jnp.sum(
                jnp.where(match, gate[r : r + 1, :], 0.0), axis=1, keepdims=True
            )

    return call(
        kernel,
        "route",
        [in_hbm(raw), in_hbm(ids), in_hbm(probs)],
        [shaped((rows, tokens), BF16), shaped((rows, 1), F32), shaped(raw.shape, BF16)],
        flops=SMALL,
        moved=SMALL,
        in_specs=[ANY] * 3,
        scratch_shapes=[
            pltpu.VMEM(ids.shape, jnp.int32),
            pltpu.VMEM(probs.shape, F32),
            pltpu.SemaphoreType.DMA((3,)),
        ],
    )


def pack(raws, sel, gate, experts, capacity, after, again=False):
    blocks = len(raws)
    columns = raws[0].shape[1]

    def kernel(*refs):
        sel_ref, gate_ref = refs[blocks : blocks + 2]
        outs = refs[blocks + 2 :]
        for b in range(blocks):
            rows = (dot(sel_ref[...], refs[b][...], NN) * gate_ref[...]).astype(BF16)
            for r, out in enumerate(outs[:experts]):
                out[b] = rows[r * capacity : (r + 1) * capacity]
        if again:
            outs[experts][...] = refs[0][...]

    return call(
        kernel,
        "pack",
        [*raws, sel, gate],
        [shaped((blocks, capacity, columns), BF16)] * experts
        + [shaped(raws[0].shape, BF16)] * again,
        after,
        flops=2 * blocks * sel.shape[0] * sel.shape[1] * columns,
        moved=6e5 * blocks,
    )


def join(pieces, after):
    experts = len(pieces)
    blocks, capacity, columns = pieces[0].shape

    def kernel(*refs):
        for r in range(experts):
            refs[experts][:, pl.ds(r * capacity, capacity), :] = refs[r][...]

    return call(
        kernel, "join", pieces, [shaped((blocks, experts * capacity, columns), BF16)], after
    )


def activations(gate_pre, up_pre, after):
    _, groups, capacity, units = gate_pre.shape
    rows = groups * capacity
    tile = 256

    def kernel(gate_hbm, up_hbm, up_factor, gate_factor, act, gate_ref, up_ref, sems):
        me = lax.axis_index("expert")
        copies = []
        for r in range(groups):
            span = pl.ds(r * capacity, capacity)
            for i, (source, target) in enumerate(((gate_hbm, gate_ref), (up_hbm, up_ref))):
                copies.append(
                    pltpu.make_async_copy(source.at[0, me ^ codes(groups)[r]], target.at[span, :], sems.at[i, r])
                )
        for copy in copies:
            copy.start()
        for copy in copies:
            copy.wait()

        def step(i, unused):
            span = pl.ds(pl.multiple_of(i * tile, tile), tile)
            a = gate_ref[:, span].astype(F32).T
            b = up_ref[:, span].astype(F32).T
            sig = 1.0 / (1.0 + jnp.exp(-a))
            swish = a * sig
            up_factor[span, :] = swish
            gate_factor[span, :] = b * sig * (1.0 + a * (1.0 - sig))
            act[span, :] = (swish * b).astype(BF16)
            return unused

        lax.fori_loop(0, units // tile, step, 0)

    return call(
        kernel,
        "activations",
        [in_hbm(gate_pre), in_hbm(up_pre)],
        [shaped((units, rows), F32), shaped((units, rows), F32), shaped((units, rows), BF16)],
        after,
        flops=ACT_FLOPS,
        moved=SMALL,
        in_specs=[ANY, ANY],
        scratch_shapes=[
            pltpu.VMEM((rows, units), BF16),
            pltpu.VMEM((rows, units), BF16),
            pltpu.SemaphoreType.DMA((2, groups)),
        ],
    )


def ring(line):
    return [*range(0, line, 2), *range(line - 1 - line % 2, 0, -2)]


def block_of(shift, line, sibling):
    cut = lax.axis_index("cuts")
    core = lax.rem(cut, 2)
    z = lax.div(cut, 2)
    order = ring(line)
    ahead = jnp.int32(0)
    for i, place in enumerate(order):
        ahead = jnp.where(z == place, order[(i + shift) % line], ahead)
    return ahead * 2 + (1 - core if sibling else core)


def hidden_part(terms, w_down, line, total, factors, after):
    _, rows, columns = terms[0][0].shape
    units = w_down.shape[1]
    count = len(terms)
    has_total = total is not None

    def kernel(*refs):
        w_ref, refs, x_refs = refs[count], refs[count + 1 :], refs[:count]
        outs = refs[has_total + len(factors) :]
        factor_refs = refs[has_total : has_total + len(factors)]
        value = refs[0][...] if has_total else 0.0
        for x_ref, (_, shifts, sibling) in zip(x_refs, terms):
            for b, shift in enumerate(shifts):
                start = pl.multiple_of(block_of(-shift, line, sibling) * columns, 128)
                value = value + dot(w_ref[0, :, pl.ds(start, columns)], x_ref[b], NT)
        if factors:
            for out, factor in zip(outs, factor_refs):
                out[...] = (value * factor[...]).astype(BF16)
        else:
            outs[0][...] = value

    return call(
        kernel,
        "hidden_part",
        [term[0] for term in terms] + [w_down] + ([total] if has_total else []) + list(factors),
        [shaped((units, rows), BF16)] * 2 if factors else [shaped((units, rows), F32)],
        after,
        moved=SMALL,
        flops=SMALL,
    )


def down_part(act, mine, theirs, shifts, line, before, out_shape, after, weight=1.0):
    blocks, rows, columns = mine.shape
    units = act.shape[0]
    split = 2
    slots = 3
    part = units // split
    steps = [(half, b) for half in range(2) for b in range(blocks)]

    def kernel(act_ref, mine_ref, theirs_ref, *refs):
        out_ref, held, sems = refs[-3:]
        copies = []
        for i, (half, b) in enumerate(steps):
            start = pl.multiple_of(block_of(-shifts[b], line, bool(half)) * columns, 128)
            now = i % slots
            x = (theirs_ref if half else mine_ref)[b]
            for j in range(split):
                if i >= slots:
                    copies[(i - slots) * split + j].wait()
                span = pl.ds(j * part, part)
                held[now, span, :] = dot(act_ref[span, :], x, NN).astype(BF16)
                copy = pltpu.make_async_copy(
                    held.at[now, span, :],
                    out_ref.at[0, span, pl.ds(start, columns)],
                    sems.at[now, j],
                )
                copy.start()
                copies.append(copy)
        for copy in copies[-slots * split :]:
            copy.wait()

    operands = [act, mine, theirs]
    if before is not None:
        operands.append(before)
    return call(
        kernel,
        "down_part",
        operands,
        [shaped(out_shape, BF16)],
        after,
        flops=weight * 4 * blocks * rows * columns * units,
        moved=weight * 4 * blocks * columns * units,
        mib=6,
        in_specs=[VMEM] * 3 + [ANY] * (len(operands) - 3),
        out_specs=[ANY],
        input_output_aliases={} if before is None else {3: 0},
        scratch_shapes=[
            pltpu.VMEM((slots, units, columns), BF16),
            pltpu.SemaphoreType.DMA((slots, split)),
        ],
    )


def slot_part(gate_grad, up_grad, w_gate, w_up, shifts, line, sibling, after):
    units, rows = gate_grad.shape
    blocks = len(shifts)
    columns = w_gate.shape[1] // (2 * line)
    tile = 256
    dtype = BF16 if sibling else F32

    def kernel(gate_ref, up_ref, wg_ref, wu_ref, out_ref):
        for b, shift in enumerate(shifts):
            base = block_of(shift, line, sibling) * columns
            for i in range(columns // tile):
                span = pl.ds(pl.multiple_of(base + i * tile, tile), tile)
                value = dot(wg_ref[0, span, :], gate_ref[...], NN)
                value = value + dot(wu_ref[0, span, :], up_ref[...], NN)
                out_ref[b, :, pl.ds(i * tile, tile)] = value.T.astype(dtype)

    return call(
        kernel,
        "slot_part",
        [gate_grad, up_grad, w_gate, w_up],
        [shaped((blocks, rows, columns), dtype)],
        after,
        flops=4 * blocks * rows * columns * units,
        moved=4 * blocks * columns * units + 4 * rows * units,
    )


def add_halves(own, arrived, experts, after):
    blocks, rows, columns = own.shape
    capacity = rows // experts

    def kernel(own_ref, other_ref, *outs):
        for b in range(blocks):
            for r in range(experts):
                span = pl.ds(r * capacity, capacity)
                value = own_ref[b, span, :] + other_ref[b, span, :].astype(F32)
                outs[r][b] = value.astype(BF16)

    return call(
        kernel,
        "add_halves",
        [own, arrived],
        [shaped((blocks, capacity, columns), BF16)] * experts,
        after,
        moved=SMALL,
        flops=SMALL,
    )


def combine(pieces, sel, others, dtypes, after):
    experts = len(pieces)
    blocks, _, columns = pieces[0].shape
    tokens = sel.shape[1]
    taken = sorted(range(experts), key=lambda r: codes(experts)[r])
    place = [taken.index(r) for r in range(experts)]
    flat = [x for group in others for x in group]

    def kernel(*refs):
        piece_refs, sel_ref = refs[:experts], refs[experts]
        other_refs = list(refs[experts + 1 : experts + 1 + len(flat)])
        out_refs = refs[experts + 1 + len(flat) :]
        for b in range(blocks):
            rows = jnp.concatenate([piece_refs[i][b] for i in place], axis=0)
            value = dot(sel_ref[...], rows, TN)
            for _ in others[b]:
                value = value + other_refs.pop(0)[...].astype(F32)
            out_refs[b][...] = value.astype(dtypes[b])

    return call(
        kernel,
        "combine",
        [*(pieces[r] for r in taken), sel, *flat],
        [shaped((tokens, columns), dtype) for dtype in dtypes],
        after,
        flops=2 * blocks * sel.shape[0] * tokens * columns,
        moved=6e5 * blocks,
    )


def slot_tables(routing, experts, capacity):
    chosen = routing.reshape(-1)
    onehot = (chosen[:, None] == jnp.arange(experts, dtype=jnp.int32)[None, :]).astype(jnp.int32)
    earlier = jnp.cumsum(onehot, axis=0) - onehot
    position = jnp.sum(earlier * onehot, axis=1)
    target = chosen * capacity + position
    source = jnp.full((experts * capacity,), chosen.shape[0], jnp.int32)
    source = source.at[target].set(jnp.arange(chosen.shape[0], dtype=jnp.int32))
    return (target, source)


def pack_rows(out_rows, gate_values, source, experts, capacity):
    columns = out_rows.shape[1]
    weighted = (gate_values[:, :, None] * out_rows[:, None, :].astype(jnp.float32)).astype(
        jnp.bfloat16
    )
    weighted = weighted.reshape(-1, columns)
    weighted = jnp.concatenate([weighted, jnp.zeros((1, columns), jnp.bfloat16)], axis=0)
    return jnp.take(weighted, source, axis=0).reshape(experts, capacity, columns)


def on_any_tiling(out_grad, gate_probs, expert_ids, gate_pre, up_pre, w_gate, w_up, w_down):
    tokens_here = expert_ids.shape[0]
    experts = lax.axis_size("expert") * w_gate.shape[0]
    groups = gate_pre.shape[1]
    capacity = gate_pre.shape[2]
    units = gate_pre.shape[3]
    local_cols = out_grad.shape[1]
    slot_rows = groups * capacity
    target, source = slot_tables(expert_ids, experts, capacity)
    down_weight = w_down[0]
    contract_last = (((1,), (1,)), ((), ()))
    contract_first = (((0,), (0,)), ((), ()))
    gate_act = gate_pre[0].reshape(slot_rows, units).astype(jnp.float32)
    up_act = up_pre[0].reshape(slot_rows, units).astype(jnp.float32)
    logistic = jax.nn.sigmoid(gate_act)
    hidden_act = (gate_act * logistic * up_act).astype(jnp.bfloat16)
    features = lax.all_gather(out_grad, "cuts", axis=1, tiled=True)
    outgoing = pack_rows(features, gate_probs, source, experts, capacity)
    routed = lax.all_to_all(outgoing, "expert", split_axis=0, concat_axis=0, tiled=True)
    routed = routed.reshape(slot_rows, routed.shape[2])
    hidden_grad = lax.dot_general(
        routed, down_weight, contract_last, preferred_element_type=jnp.float32
    )
    down_grad = lax.dot_general(
        hidden_act, routed, contract_first, preferred_element_type=jnp.float32
    )
    w_down_grad = down_grad.astype(jnp.bfloat16)[None]
    up_grad = (hidden_grad * gate_act * logistic).astype(jnp.bfloat16)
    gate_grad = (hidden_grad * up_act * logistic * (1.0 + gate_act * (1.0 - logistic))).astype(
        jnp.bfloat16
    )
    gate_weight = w_gate[0]
    up_weight = w_up[0]
    partial_value = lax.dot_general(
        gate_weight, gate_grad, contract_last, preferred_element_type=jnp.float32
    )
    partial_value = partial_value + lax.dot_general(
        up_weight, up_grad, contract_last, preferred_element_type=jnp.float32
    )
    summed = lax.psum_scatter(
        lax.optimization_barrier(partial_value.astype(jnp.bfloat16))
        .astype(jnp.float32)
        .astype(jnp.bfloat16),
        "cuts",
        scatter_dimension=0,
        tiled=True,
    ).astype(jnp.float32)
    summed = summed.reshape(local_cols, groups, capacity)
    returned = lax.all_to_all(
        summed.astype(jnp.bfloat16), "expert", split_axis=1, concat_axis=1, tiled=True
    ).astype(summed.dtype)
    flat_back = returned.reshape(local_cols, experts * capacity)
    picked = jnp.take(flat_back, target, axis=1).reshape(local_cols, tokens_here, -1)
    input_grad = jnp.sum(picked, axis=2)
    return (input_grad.T.astype(jnp.bfloat16), w_down_grad)


def on_device(out_grad, gate_probs, expert_ids, gate_pre, up_pre, w_gate, w_up, w_down):
    experts = lax.axis_size("expert")
    cuts = lax.axis_size("cuts")
    line = cuts // 2
    capacity = gate_pre.shape[2]
    if out_grad.shape[1] % 256 or gate_pre.shape[3] % 256 or capacity % 16 or cuts != 8:
        return on_any_tiling(
            out_grad, gate_probs, expert_ids, gate_pre, up_pre, w_gate, w_up, w_down
        )

    def along(x, shift):
        order = ring(line)
        pairs = [
            (2 * order[i] + core, 2 * order[(i + shift) % line] + core)
            for i in range(line)
            for core in range(2)
        ]
        return lax.ppermute(x, "cuts", pairs)

    def swap(x):
        return lax.ppermute(x, "cuts", [(i, i ^ 1) for i in range(cuts)])

    def exchange(pieces):
        return [
            lax.ppermute(piece, "expert", [(i, i ^ code) for i in range(experts)]) if code else piece
            for piece, code in zip(pieces, codes(experts))
        ]

    raw1 = along(out_grad, 1)
    raw2 = along(raw1, 1)
    raw3 = along(out_grad, 3)
    one, two = [0, 1], [3, 2]
    sel, gate, own, t = route(out_grad, expert_ids.T, gate_probs.T, experts, capacity)
    *pieces, t = pack([own, raw1], sel, gate, experts, capacity, [t])
    pieces = exchange(pieces)
    *pieces2, t = pack([raw3, raw2], sel, gate, experts, capacity, [t])
    pieces2 = exchange(pieces2)
    up_factor, gate_factor, act, t = activations(gate_pre, up_pre, [t])
    mine1, t = join(pieces, [t])
    theirs1 = swap(mine1)
    mine2, t = join(pieces2, [t])
    theirs2 = swap(mine2)
    total, t = hidden_part(
        [(mine1, one, False), (theirs1, one, True), (mine2, two, False)],
        w_down, line, None, (), [t],
    )
    gate_grad, up_grad, t = hidden_part(
        [(theirs2, two, True)], w_down, line, total, (gate_factor, up_factor), [t, w_gate]
    )

    first, last = [2, 3], [1, 0]
    back = functools.partial(slot_part, gate_grad, up_grad, w_gate, w_up)
    def exchanged(shifts, t):
        part, t = back(shifts, line, True, [t])
        arrived = swap(part)
        part, t = back(shifts, line, False, [t])
        *pieces, t = add_halves(part, arrived, experts, [t])
        return exchange(pieces), t

    got1, t = exchanged(first, t)
    got2, t = exchanged(last, t)
    part2, part3, t = combine(got1, sel, [[], []], [BF16, BF16], [t])
    landed2 = along(part2, 1)
    landed3 = along(part3, 3)
    down, t = down_part(act, mine1, theirs1, one, line, None, w_down.shape, [t])
    part1, part0, t = combine(got2, sel, [[landed2], []], [BF16, F32], [t])
    landed1 = along(part1, 1)
    down, t = down_part(act, mine2, theirs2, two, line, down, w_down.shape, [t], DOWN_WEIGHT)
    result = (part0 + landed3.astype(F32) + landed1.astype(F32)).astype(BF16)
    return result, down


def solution(mesh):
    return jax.shard_map(
        on_device,
        mesh=mesh,
        in_specs=(
            P("expert", "cuts"),
            P("expert", None),
            P("expert", None),
            P("expert", None, None, "cuts"),
            P("expert", None, None, "cuts"),
            P("expert", None, "cuts"),
            P("expert", None, "cuts"),
            P("expert", "cuts", None),
        ),
        out_specs=(P("expert", "cuts"), P("expert", "cuts", None)),
        check_vma=False,
    )
```

```python
import functools
import jax
import jax.numpy as jnp
from jax import lax
from jax.experimental import pallas as pl
from jax.experimental.pallas import tpu as pltpu
from jax.sharding import PartitionSpec as P

BF16 = jnp.bfloat16
F32 = jnp.float32
VMEM = pl.BlockSpec(memory_space=pltpu.VMEM)
ANY = pl.BlockSpec(memory_space=pl.ANY)
NT = (((1,), (1,)), ((), ()))
TN = (((0,), (0,)), ((), ()))
NN = (((1,), (0,)), ((), ()))
MIB = 1 << 20
ACT_FLOPS = 1.2e10
SMALL = 1e3
DOWN_WEIGHT = 0.0


def dot(a, b, dims):
    return lax.dot_general(a, b, dims, preferred_element_type=F32)


def shaped(shape, dtype):
    return jax.ShapeDtypeStruct(shape, dtype)


def in_hbm(x):
    return pltpu.with_memory_space_constraint(x, pltpu.HBM)


def call(kernel, name, operands, out_shape, after=(), flops=0, moved=0, mib=4, out_specs=None, **more):
    count, extra, results = len(operands), len(after), len(out_shape)

    def body(*refs):
        outs = refs[count + extra :]
        kernel(*refs[:count], *outs[:results], *outs[results + 1 :])
        outs[results][...] = jnp.zeros((8, 128), F32)

    out_shape = list(out_shape) + [shaped((8, 128), F32)]
    out_specs = list(out_specs or [VMEM] * results) + [VMEM]
    specs = more.pop("in_specs", [VMEM] * count)
    return pl.pallas_call(
        body,
        out_shape=out_shape,
        in_specs=list(specs) + [VMEM] * extra,
        out_specs=out_specs,
        compiler_params=pltpu.CompilerParams(vmem_limit_bytes=mib * MIB),
        cost_estimate=pl.CostEstimate(
            flops=int(flops), bytes_accessed=int(moved), transcendentals=0
        ),
        name=name,
        **more,
    )(*operands, *after)


def codes(experts):
    return list(range(experts))


def route(raw, ids, probs, experts, capacity):
    tokens = ids.shape[1]
    lines = max(8, experts)
    rows = experts * capacity

    def kernel(raw_hbm, ids_hbm, probs_hbm, sel_ref, gate_ref, own_ref, ids_ref, probs_ref, sems):
        copies = [
            pltpu.make_async_copy(ids_hbm, ids_ref, sems.at[0]),
            pltpu.make_async_copy(probs_hbm, probs_ref, sems.at[1]),
            pltpu.make_async_copy(raw_hbm, own_ref, sems.at[2]),
        ]
        for copy in copies:
            copy.start()
        before = lax.broadcasted_iota(jnp.int32, (tokens, tokens), 0)
        here = lax.broadcasted_iota(jnp.int32, (tokens, tokens), 1)
        earlier = (before < here).astype(F32).astype(BF16)
        slot = lax.broadcasted_iota(jnp.int32, (capacity, tokens), 0).astype(F32)
        line = lax.broadcasted_iota(jnp.int32, (lines, tokens), 0)
        expert = jnp.full((lines, tokens), experts, jnp.int32)
        for r, code in enumerate(codes(experts)):
            expert = jnp.where(line == r, lax.axis_index("expert") ^ code, expert)
        for copy in copies:
            copy.wait()
        first = (ids_ref[0:1, :] == expert).astype(F32)
        second = (ids_ref[1:2, :] == expert).astype(F32)
        hit = first + second
        place = dot(hit.astype(BF16), earlier, NN)
        place = jnp.where(hit > 0.0, place, -1.0)
        gate = first * probs_ref[0:1, :] + second * probs_ref[1:2, :]
        for r in range(experts):
            match = place[r : r + 1, :] == slot
            span = pl.ds(r * capacity, capacity)
            sel_ref[span, :] = jnp.where(match, 1.0, 0.0).astype(BF16)
            gate_ref[span, :] = jnp.sum(
                jnp.where(match, gate[r : r + 1, :], 0.0), axis=1, keepdims=True
            )

    return call(
        kernel,
        "route",
        [in_hbm(raw), in_hbm(ids), in_hbm(probs)],
        [shaped((rows, tokens), BF16), shaped((rows, 1), F32), shaped(raw.shape, BF16)],
        flops=SMALL,
        moved=SMALL,
        in_specs=[ANY] * 3,
        scratch_shapes=[
            pltpu.VMEM(ids.shape, jnp.int32),
            pltpu.VMEM(probs.shape, F32),
            pltpu.SemaphoreType.DMA((3,)),
        ],
    )


def pack(raws, sel, gate, experts, capacity, after, again=False):
    blocks = len(raws)
    columns = raws[0].shape[1]

    def kernel(*refs):
        sel_ref, gate_ref = refs[blocks : blocks + 2]
        outs = refs[blocks + 2 :]
        for b in range(blocks):
            rows = (dot(sel_ref[...], refs[b][...], NN) * gate_ref[...]).astype(BF16)
            for r, out in enumerate(outs[:experts]):
                out[b] = rows[r * capacity : (r + 1) * capacity]
        if again:
            outs[experts][...] = refs[0][...]

    return call(
        kernel,
        "pack",
        [*raws, sel, gate],
        [shaped((blocks, capacity, columns), BF16)] * experts
        + [shaped(raws[0].shape, BF16)] * again,
        after,
        flops=2 * blocks * sel.shape[0] * sel.shape[1] * columns,
        moved=6e5 * blocks,
    )


def join(pieces, after):
    experts = len(pieces)
    blocks, capacity, columns = pieces[0].shape

    def kernel(*refs):
        for r in range(experts):
            refs[experts][:, pl.ds(r * capacity, capacity), :] = refs[r][...]

    return call(
        kernel, "join", pieces, [shaped((blocks, experts * capacity, columns), BF16)], after
    )


def activations(gate_pre, up_pre, after):
    _, groups, capacity, units = gate_pre.shape
    rows = groups * capacity
    tile = 256

    def kernel(gate_hbm, up_hbm, up_factor, gate_factor, act, gate_ref, up_ref, sems):
        me = lax.axis_index("expert")
        copies = []
        for r in range(groups):
            span = pl.ds(r * capacity, capacity)
            for i, (source, target) in enumerate(((gate_hbm, gate_ref), (up_hbm, up_ref))):
                copies.append(
                    pltpu.make_async_copy(source.at[0, me ^ codes(groups)[r]], target.at[span, :], sems.at[i, r])
                )
        for copy in copies:
            copy.start()
        for copy in copies:
            copy.wait()

        def step(i, unused):
            span = pl.ds(pl.multiple_of(i * tile, tile), tile)
            a = gate_ref[:, span].astype(F32).T
            b = up_ref[:, span].astype(F32).T
            sig = 1.0 / (1.0 + jnp.exp(-a))
            swish = a * sig
            up_factor[span, :] = swish
            gate_factor[span, :] = b * sig * (1.0 + a * (1.0 - sig))
            act[span, :] = (swish * b).astype(BF16)
            return unused

        lax.fori_loop(0, units // tile, step, 0)

    return call(
        kernel,
        "activations",
        [in_hbm(gate_pre), in_hbm(up_pre)],
        [shaped((units, rows), F32), shaped((units, rows), F32), shaped((units, rows), BF16)],
        after,
        flops=ACT_FLOPS,
        moved=SMALL,
        in_specs=[ANY, ANY],
        scratch_shapes=[
            pltpu.VMEM((rows, units), BF16),
            pltpu.VMEM((rows, units), BF16),
            pltpu.SemaphoreType.DMA((2, groups)),
        ],
    )


def ring(line):
    return [*range(0, line, 2), *range(line - 1 - line % 2, 0, -2)]


def block_of(shift, line, sibling):
    cut = lax.axis_index("cuts")
    core = lax.rem(cut, 2)
    z = lax.div(cut, 2)
    order = ring(line)
    ahead = jnp.int32(0)
    for i, place in enumerate(order):
        ahead = jnp.where(z == place, order[(i + shift) % line], ahead)
    return ahead * 2 + (1 - core if sibling else core)


def hidden_part(terms, w_down, line, total, factors, after):
    _, rows, columns = terms[0][0].shape
    units = w_down.shape[1]
    count = len(terms)
    has_total = total is not None

    def kernel(*refs):
        w_ref, refs, x_refs = refs[count], refs[count + 1 :], refs[:count]
        outs = refs[has_total + len(factors) :]
        factor_refs = refs[has_total : has_total + len(factors)]
        value = refs[0][...] if has_total else 0.0
        for x_ref, (_, shifts, sibling) in zip(x_refs, terms):
            for b, shift in enumerate(shifts):
                start = pl.multiple_of(block_of(-shift, line, sibling) * columns, 128)
                value = value + dot(w_ref[0, :, pl.ds(start, columns)], x_ref[b], NT)
        if factors:
            for out, factor in zip(outs, factor_refs):
                out[...] = (value * factor[...]).astype(BF16)
        else:
            outs[0][...] = value

    return call(
        kernel,
        "hidden_part",
        [term[0] for term in terms] + [w_down] + ([total] if has_total else []) + list(factors),
        [shaped((units, rows), BF16)] * 2 if factors else [shaped((units, rows), F32)],
        after,
        moved=SMALL,
        flops=SMALL,
    )


def down_part(act, mine, theirs, shifts, line, before, out_shape, after, weight=1.0):
    blocks, rows, columns = mine.shape
    units = act.shape[0]
    split = 2
    slots = 3
    part = units // split
    steps = [(half, b) for half in range(2) for b in range(blocks)]

    def kernel(act_ref, mine_ref, theirs_ref, *refs):
        out_ref, held, sems = refs[-3:]
        copies = []
        for i, (half, b) in enumerate(steps):
            start = pl.multiple_of(block_of(-shifts[b], line, bool(half)) * columns, 128)
            now = i % slots
            x = (theirs_ref if half else mine_ref)[b]
            for j in range(split):
                if i >= slots:
                    copies[(i - slots) * split + j].wait()
                span = pl.ds(j * part, part)
                held[now, span, :] = dot(act_ref[span, :], x, NN).astype(BF16)
                copy = pltpu.make_async_copy(
                    held.at[now, span, :],
                    out_ref.at[0, span, pl.ds(start, columns)],
                    sems.at[now, j],
                )
                copy.start()
                copies.append(copy)
        for copy in copies[-slots * split :]:
            copy.wait()

    operands = [act, mine, theirs]
    if before is not None:
        operands.append(before)
    return call(
        kernel,
        "down_part",
        operands,
        [shaped(out_shape, BF16)],
        after,
        flops=weight * 4 * blocks * rows * columns * units,
        moved=weight * 4 * blocks * columns * units,
        mib=6,
        in_specs=[VMEM] * 3 + [ANY] * (len(operands) - 3),
        out_specs=[ANY],
        input_output_aliases={} if before is None else {3: 0},
        scratch_shapes=[
            pltpu.VMEM((slots, units, columns), BF16),
            pltpu.SemaphoreType.DMA((slots, split)),
        ],
    )


def slot_part(gate_grad, up_grad, w_gate, w_up, shifts, line, sibling, after):
    units, rows = gate_grad.shape
    blocks = len(shifts)
    columns = w_gate.shape[1] // (2 * line)
    tile = 256
    dtype = BF16 if sibling else F32

    def kernel(gate_ref, up_ref, wg_ref, wu_ref, out_ref):
        for b, shift in enumerate(shifts):
            base = block_of(shift, line, sibling) * columns
            for i in range(columns // tile):
                span = pl.ds(pl.multiple_of(base + i * tile, tile), tile)
                value = dot(wg_ref[0, span, :], gate_ref[...], NN)
                value = value + dot(wu_ref[0, span, :], up_ref[...], NN)
                out_ref[b, :, pl.ds(i * tile, tile)] = value.T.astype(dtype)

    return call(
        kernel,
        "slot_part",
        [gate_grad, up_grad, w_gate, w_up],
        [shaped((blocks, rows, columns), dtype)],
        after,
        flops=4 * blocks * rows * columns * units,
        moved=4 * blocks * columns * units + 4 * rows * units,
    )


def add_halves(own, arrived, experts, after):
    blocks, rows, columns = own.shape
    capacity = rows // experts

    def kernel(own_ref, other_ref, *outs):
        for b in range(blocks):
            for r in range(experts):
                span = pl.ds(r * capacity, capacity)
                value = own_ref[b, span, :] + other_ref[b, span, :].astype(F32)
                outs[r][b] = value.astype(BF16)

    return call(
        kernel,
        "add_halves",
        [own, arrived],
        [shaped((blocks, capacity, columns), BF16)] * experts,
        after,
        moved=SMALL,
        flops=SMALL,
    )


def combine(pieces, sel, others, dtypes, after):
    experts = len(pieces)
    blocks, _, columns = pieces[0].shape
    tokens = sel.shape[1]
    flat = [x for group in others for x in group]

    def kernel(*refs):
        piece_refs, sel_ref = refs[:experts], refs[experts]
        other_refs = list(refs[experts + 1 : experts + 1 + len(flat)])
        out_refs = refs[experts + 1 + len(flat) :]
        for b in range(blocks):
            rows = jnp.concatenate([piece[b] for piece in piece_refs], axis=0)
            value = dot(sel_ref[...], rows, TN)
            for _ in others[b]:
                value = value + other_refs.pop(0)[...].astype(F32)
            out_refs[b][...] = value.astype(dtypes[b])

    return call(
        kernel,
        "combine",
        [*pieces, sel, *flat],
        [shaped((tokens, columns), dtype) for dtype in dtypes],
        after,
        flops=2 * blocks * sel.shape[0] * tokens * columns,
        moved=6e5 * blocks,
    )


def slot_tables(routing, experts, capacity):
    chosen = routing.reshape(-1)
    onehot = (chosen[:, None] == jnp.arange(experts, dtype=jnp.int32)[None, :]).astype(jnp.int32)
    earlier = jnp.cumsum(onehot, axis=0) - onehot
    position = jnp.sum(earlier * onehot, axis=1)
    target = chosen * capacity + position
    source = jnp.full((experts * capacity,), chosen.shape[0], jnp.int32)
    source = source.at[target].set(jnp.arange(chosen.shape[0], dtype=jnp.int32))
    return (target, source)


def pack_rows(out_rows, gate_values, source, experts, capacity):
    columns = out_rows.shape[1]
    weighted = (gate_values[:, :, None] * out_rows[:, None, :].astype(jnp.float32)).astype(
        jnp.bfloat16
    )
    weighted = weighted.reshape(-1, columns)
    weighted = jnp.concatenate([weighted, jnp.zeros((1, columns), jnp.bfloat16)], axis=0)
    return jnp.take(weighted, source, axis=0).reshape(experts, capacity, columns)


def on_any_tiling(out_grad, gate_probs, expert_ids, gate_pre, up_pre, w_gate, w_up, w_down):
    tokens_here = expert_ids.shape[0]
    experts = lax.axis_size("expert") * w_gate.shape[0]
    groups = gate_pre.shape[1]
    capacity = gate_pre.shape[2]
    units = gate_pre.shape[3]
    local_cols = out_grad.shape[1]
    slot_rows = groups * capacity
    target, source = slot_tables(expert_ids, experts, capacity)
    down_weight = w_down[0]
    contract_last = (((1,), (1,)), ((), ()))
    contract_first = (((0,), (0,)), ((), ()))
    gate_act = gate_pre[0].reshape(slot_rows, units).astype(jnp.float32)
    up_act = up_pre[0].reshape(slot_rows, units).astype(jnp.float32)
    logistic = jax.nn.sigmoid(gate_act)
    hidden_act = (gate_act * logistic * up_act).astype(jnp.bfloat16)
    features = lax.all_gather(out_grad, "cuts", axis=1, tiled=True)
    outgoing = pack_rows(features, gate_probs, source, experts, capacity)
    routed = lax.all_to_all(outgoing, "expert", split_axis=0, concat_axis=0, tiled=True)
    routed = routed.reshape(slot_rows, routed.shape[2])
    hidden_grad = lax.dot_general(
        routed, down_weight, contract_last, preferred_element_type=jnp.float32
    )
    down_grad = lax.dot_general(
        hidden_act, routed, contract_first, preferred_element_type=jnp.float32
    )
    w_down_grad = down_grad.astype(jnp.bfloat16)[None]
    up_grad = (hidden_grad * gate_act * logistic).astype(jnp.bfloat16)
    gate_grad = (hidden_grad * up_act * logistic * (1.0 + gate_act * (1.0 - logistic))).astype(
        jnp.bfloat16
    )
    gate_weight = w_gate[0]
    up_weight = w_up[0]
    partial_value = lax.dot_general(
        gate_weight, gate_grad, contract_last, preferred_element_type=jnp.float32
    )
    partial_value = partial_value + lax.dot_general(
        up_weight, up_grad, contract_last, preferred_element_type=jnp.float32
    )
    summed = lax.psum_scatter(
        lax.optimization_barrier(partial_value.astype(jnp.bfloat16))
        .astype(jnp.float32)
        .astype(jnp.bfloat16),
        "cuts",
        scatter_dimension=0,
        tiled=True,
    ).astype(jnp.float32)
    summed = summed.reshape(local_cols, groups, capacity)
    returned = lax.all_to_all(
        summed.astype(jnp.bfloat16), "expert", split_axis=1, concat_axis=1, tiled=True
    ).astype(summed.dtype)
    flat_back = returned.reshape(local_cols, experts * capacity)
    picked = jnp.take(flat_back, target, axis=1).reshape(local_cols, tokens_here, -1)
    input_grad = jnp.sum(picked, axis=2)
    return (input_grad.T.astype(jnp.bfloat16), w_down_grad)


def on_device(out_grad, gate_probs, expert_ids, gate_pre, up_pre, w_gate, w_up, w_down):
    experts = lax.axis_size("expert")
    cuts = lax.axis_size("cuts")
    line = cuts // 2
    capacity = gate_pre.shape[2]
    if out_grad.shape[1] % 256 or gate_pre.shape[3] % 256 or capacity % 16 or cuts != 8:
        return on_any_tiling(
            out_grad, gate_probs, expert_ids, gate_pre, up_pre, w_gate, w_up, w_down
        )

    def along(x, shift):
        order = ring(line)
        pairs = [
            (2 * order[i] + core, 2 * order[(i + shift) % line] + core)
            for i in range(line)
            for core in range(2)
        ]
        return lax.ppermute(x, "cuts", pairs)

    def swap(x):
        return lax.ppermute(x, "cuts", [(i, i ^ 1) for i in range(cuts)])

    def exchange(pieces):
        return [
            lax.ppermute(piece, "expert", [(i, i ^ code) for i in range(experts)]) if code else piece
            for piece, code in zip(pieces, codes(experts))
        ]

    raw1 = along(out_grad, 1)
    raw2 = along(raw1, 1)
    raw3 = along(out_grad, 3)
    one, two = [0, 1], [3, 2]
    sel, gate, own, t = route(out_grad, expert_ids.T, gate_probs.T, experts, capacity)
    *pieces, t = pack([own, raw1], sel, gate, experts, capacity, [t])
    pieces = exchange(pieces)
    *pieces2, t = pack([raw3, raw2], sel, gate, experts, capacity, [t])
    pieces2 = exchange(pieces2)
    up_factor, gate_factor, act, t = activations(gate_pre, up_pre, [t])
    mine1, t = join(pieces, [t])
    theirs1 = swap(mine1)
    mine2, t = join(pieces2, [t])
    theirs2 = swap(mine2)
    total, t = hidden_part(
        [(mine1, one, False), (theirs1, one, True), (mine2, two, False)],
        w_down, line, None, (), [t],
    )
    gate_grad, up_grad, t = hidden_part(
        [(theirs2, two, True)], w_down, line, total, (gate_factor, up_factor), [t, w_gate]
    )

    first, last = [2, 3], [1, 0]
    back = functools.partial(slot_part, gate_grad, up_grad, w_gate, w_up)
    def halves(shifts, t):
        part, t = back(shifts, line, True, [t])
        return swap(part), t

    other1, t = halves(first, t)
    part, t = back(first, line, False, [t])
    *pieces, t = add_halves(part, other1, experts, [t])
    got1 = exchange(pieces)
    other2, t = halves(last, t)
    down, t = down_part(act, mine1, theirs1, one, line, None, w_down.shape, [t])
    part, t = back(last, line, False, [t])
    *pieces, t = add_halves(part, other2, experts, [t])
    got2 = exchange(pieces)
    part2, part3, t = combine(got1, sel, [[], []], [BF16, BF16], [t])
    landed2 = along(part2, 1)
    landed3 = along(part3, 3)
    part1, part0, t = combine(got2, sel, [[landed2], []], [BF16, F32], [t])
    landed1 = along(part1, 1)
    down, t = down_part(act, mine2, theirs2, two, line, down, w_down.shape, [t], DOWN_WEIGHT)
    result = (part0 + landed3.astype(F32) + landed1.astype(F32)).astype(BF16)
    return result, down


def solution(mesh):
    return jax.shard_map(
        on_device,
        mesh=mesh,
        in_specs=(
            P("expert", "cuts"),
            P("expert", None),
            P("expert", None),
            P("expert", None, None, "cuts"),
            P("expert", None, None, "cuts"),
            P("expert", None, "cuts"),
            P("expert", None, "cuts"),
            P("expert", "cuts", None),
        ),
        out_specs=(P("expert", "cuts"), P("expert", "cuts", None)),
        check_vma=False,
    )
```
